512 devices in a mesh: dp: 16 (over z), expert: 32 (over x, y, core).
Axes of the slice: x: 4, y: 4, z: 16, core: 2. Of those that a mesh axis runs over, the one named last changes fastest.
Arguments:
- tokens: bfloat16 [65536, 2048], P(('dp', 'expert')), may hold values from -6 to 6
- route_gates: float32 [65536, 3], P(('dp', 'expert')), may hold values from 0.1 to 1
- expert_ids: int32 [65536, 3], P(('dp', 'expert')), may hold values from 0 to 31, all different within a row; in each aligned block of 128 rows (0 to 127, 128 to 255, ...) at most 14 rows name the same one
- owner_now: int32 [32], replicated, may hold values from 0 to 31, as said below
- owner_next: int32 [32], replicated, may hold values from 0 to 31, as said below
- out_grad: bfloat16 [65536, 2048], P(('dp', 'expert')), may hold values from -6 to 6
- expert_weights: bfloat16 [32, 2048, 1152], P('expert', 'dp'), may hold values from -0.125 to 0.125
- first_moment: bfloat16 [32, 2048, 1152], P('expert', 'dp'), may hold values from -12 to 12
- second_moment: bfloat16 [32, 2048, 1152], P('expert', 'dp'), may hold values from 5 to 80
Outputs:
- moe_out: bfloat16 [65536, 2048], P(('dp', 'expert'))
- tokens_grad: bfloat16 [65536, 2048], P(('dp', 'expert'))
- gate_grads: float32 [65536, 3], P(('dp', 'expert'))
- new_weights: bfloat16 [32, 2048, 1152], P('expert', 'dp')
- new_first: bfloat16 [32, 2048, 1152], P('expert', 'dp')
- new_second: bfloat16 [32, 2048, 1152], P('expert', 'dp')
The draws below stay inside these ranges and needn't reach their ends.
Inputs may be any that keep to these rules, and one draw needn't show every extreme that they name: `expert_ids`: within the 128 tokens of one device no expert is named by more than 14 routes, and in some such block one expert is named by exactly 14. `owner_now`: A permutation of the 32 indices of expert. `owner_next`: A permutation that equals owner_now except on 16 experts, which exchange their holders among themselves, none keeping its own.
All inputs are finite; a program needn't handle non-finite values.
Results may differ from the reference program's by a relative error of at most 0.007.
Values may be sent and summed in bfloat16 or wider, within the bound.
A program may use at most 64 MiB of HBM per device.

```python
import math
import jax
import jax.numpy as jnp
import numpy as np
from jax import lax

D = 2048
HID = 384
ROUTES = 3
TOK_DEV = 128
TOKENS = 65536
EXPERTS = 32
CAP = 14
HOT = 16
N_DP = 16
N_EXPERT = 32


def placement_tables(key):
    first_key = jax.random.fold_in(key, 11)
    second_key = jax.random.fold_in(key, 23)
    current = jax.random.permutation(first_key, N_EXPERT).astype(jnp.int32)
    hot_order = jax.random.permutation(second_key, N_EXPERT).astype(jnp.int32)
    hot_set = hot_order[:HOT]
    rolled = jnp.roll(hot_set, 1)
    following = current.at[hot_set].set(current[rolled])
    return (current, following)


def draw_owner_now(key, part):
    return placement_tables(key)[0]


def draw_owner_next(key, part):
    return placement_tables(key)[1]


def steps_of(key, shape, pieces, least, high):
    factor_of, own = 1.0, jax.random.fold_in(key, 6)
    for dim, shards_of in pieces:
        heights = jnp.exp(jax.random.uniform(jax.random.fold_in(own, dim), (shards_of,), jnp.float32, least / len(pieces), high / len(pieces)))
        factor_of = factor_of * jnp.repeat(heights, shape[dim] // shards_of).reshape([-1 if axis == dim else 1 for axis in range(len(shape))])
    return factor_of


def routed_block(rng, own, number, rows, number_of, top, most, skew):
    order = jax.random.permutation(rng, number_of)
    crowded, ordinary = portions_of(number_of, rows * top, most, skew, True), portions_of(number_of, rows * top, most, skew, False)
    places = jnp.arange(number_of)

    def named(tallies, turn):
        used = int((tallies > 0).sum())
        fixed = max(1, used // 4)
        passed = fixed + (places - fixed + turn * (used - fixed)) % max(1, number_of - fixed)
        return jnp.zeros((number_of,), jnp.int32).at[order[jnp.where(places < fixed, places, passed)]].set(jnp.asarray(tallies, jnp.int32))

    tallies = jnp.where(number % 4 == 0, named(crowded, number // 4), named(ordinary, number - number // 4 - 1))
    mixed = jax.random.permutation(jax.random.fold_in(own, 3), number_of)
    giver, taker = mixed[0:number_of // 2 * 2:2], mixed[1:number_of // 2 * 2:2]
    room = jnp.minimum(tallies[giver] - 1, most - tallies[taker]) // 2
    room = jnp.where((giver == order[0]) | (taker == order[0]) | (tallies[taker] == 0), 0, jnp.maximum(room, 0))
    passed = jax.random.randint(jax.random.fold_in(own, 4), (number_of // 2,), 0, 1 << 20) % (room + 1)
    tallies = tallies.at[giver].add(-passed).at[taker].add(passed)
    items = jnp.searchsorted(jnp.cumsum(tallies), jnp.arange(rows * top), side="right").astype(jnp.int32)
    listing = items.reshape(top, rows).T
    listing = listing[jax.random.permutation(jax.random.fold_in(own, 1), rows)]
    turn = jax.random.randint(jax.random.fold_in(own, 2), (rows, 1), 0, top)
    return jnp.take_along_axis(listing, (jnp.arange(top)[None, :] + turn) % top, axis=1)


def portions_of(count, total, limit, slope, full):
    portions = [(1 << 20) // math.isqrt(grade ** slope) + 1 for grade in range(1, count + 1)]
    largest = limit if full else min(limit, max(-(-total // count), total * portions[0] // sum(portions)))
    least = 1 if total - largest >= count - 1 else 0
    given, rest = [largest] + [least] * (count - 1), total - largest - least * (count - 1)
    while rest > 0:
        movable = [i for i in range(1, count) if given[i] < largest] or [i for i in range(1, count) if given[i] < limit]
        whole, remaining = sum([portions[i] for i in movable]), rest
        for i in movable:
            extra = min(limit - given[i], max(1, remaining * portions[i] // whole), rest)
            given[i] = given[i] + extra
            rest = rest - extra
    return np.array(given)


def normal_values(stream_key, extent, spread, most, cuts=(), kind=jnp.bfloat16):
    loudness = steps_of(stream_key, extent, cuts, -0.22, 0.18) if cuts else 1.0
    entries = jax.random.normal(stream_key, extent, jnp.float32) * spread * loudness
    return jnp.minimum(jnp.maximum(entries, -most), most).astype(kind)


def setup_inputs(seed: int = 0) -> dict:
    streams_of = jax.random.split(jax.random.key(seed), 10)
    tokens = normal_values(streams_of[0], (TOKENS, D), 1.0, 6.0, ((0, 512),))
    route_gates = jnp.clip(0.1 + 0.9 * jax.random.uniform(streams_of[1], (TOKENS, ROUTES), jnp.float32) ** steps_of(streams_of[1], (TOKENS, ROUTES), ((0, 512),), -0.2, 0.2), 0.1, 1.0)
    expert_ids_keys = jax.random.split(jax.random.fold_in(streams_of[2], 1), TOKENS // TOK_DEV)
    expert_ids_turns = jax.random.permutation(jax.random.fold_in(streams_of[2], 3), TOKENS // TOK_DEV)
    expert_ids = jax.vmap(lambda own, number: routed_block(jax.random.fold_in(streams_of[2], 2), own, number, TOK_DEV, EXPERTS, ROUTES, CAP, 1))(expert_ids_keys, expert_ids_turns).reshape((TOKENS, ROUTES))
    owner_now = draw_owner_now(jax.random.fold_in(streams_of[9], 71), 0)
    owner_next = draw_owner_next(jax.random.fold_in(streams_of[9], 71), 0)
    out_grad = normal_values(streams_of[5], (TOKENS, D), 1.0, 6.0, ((0, 512),))
    expert_weights = normal_values(streams_of[6], (EXPERTS, D, 3 * HID), D ** -0.5, 0.125, ((0, 32), (1, 16)))
    first_moment = normal_values(streams_of[7], (EXPERTS, D, 3 * HID), 2.0, 12.0, ((0, 32), (1, 16)))
    second_moment = jnp.clip(jnp.exp(math.log(80.0) - 2.7725887 * jax.random.uniform(streams_of[8], (EXPERTS, D, 3 * HID), jnp.float32) ** steps_of(streams_of[8], (EXPERTS, D, 3 * HID), ((0, 32), (1, 16)), -0.2, 0.2)), 5.0, 80.0).astype(jnp.bfloat16)
    return dict(tokens=tokens, route_gates=route_gates, expert_ids=expert_ids, owner_now=owner_now, owner_next=owner_next, out_grad=out_grad, expert_weights=expert_weights, first_moment=first_moment, second_moment=second_moment)


beta_one = 0.9
beta_two = 0.95
learn_rate = 0.003
adam_eps = 1e-08

def route_slots(expert_ids, owner_now, capacity):
    tok_count, routes = expert_ids.shape
    experts = owner_now.shape[0]
    one_hot = (expert_ids[:, :, None] == jnp.arange(experts, dtype=jnp.int32)[None, None, :]).astype(jnp.int32)
    slot_index = lax.optimization_barrier(jnp.sum(one_hot * owner_now[None, None, :], axis=2)).astype(jnp.int32)
    flat_hits = one_hot.reshape(tok_count * routes, experts)
    earlier = jnp.cumsum(flat_hits, axis=0, dtype=jnp.int32) - flat_hits
    position = lax.optimization_barrier(jnp.sum(earlier * flat_hits, axis=1)).astype(jnp.int32).reshape(tok_count, routes)
    return (slot_index * capacity + position).astype(jnp.int32)

def slot_rows(destination, route_gates, slot_total):
    tok_count, routes = destination.shape
    matches = destination.reshape(1, tok_count * routes) == jnp.arange(slot_total, dtype=jnp.int32)[:, None]
    token_of = (jnp.arange(tok_count * routes, dtype=jnp.int32) // routes)[None, :]
    row_token = lax.optimization_barrier(jnp.sum(jnp.where(matches, token_of, 0), axis=1)).astype(jnp.int32)
    row_live = jnp.any(matches, axis=1)
    row_gate = lax.optimization_barrier(jnp.sum(jnp.where(matches, route_gates.reshape(1, -1), 0.0), axis=1))
    return (row_token, row_live, row_gate)

def owner_sources(owner_now, owner_next):
    experts = owner_now.shape[0]
    matches = owner_next[None, :] == jnp.arange(experts, dtype=jnp.int32)[:, None]
    return lax.optimization_barrier(jnp.sum(jnp.where(matches, owner_now[None, :], 0), axis=1)).astype(jnp.int32)

def expert_pass(row_inputs, route_grad, weights):
    hidden = weights.shape[1] // 3
    weight_in = weights[:, :2 * hidden]
    weight_down = weights[:, 2 * hidden:]
    gate_up = jnp.dot(row_inputs, weight_in, preferred_element_type=jnp.float32)
    gate_part = gate_up[:, :hidden]
    up_part = gate_up[:, hidden:]
    sigmoid_gate = jax.nn.sigmoid(gate_part)
    activation = (gate_part * sigmoid_gate * up_part).astype(jnp.bfloat16)
    routed = lax.dot_general(activation, weight_down, (((1,), (1,)), ((), ())), preferred_element_type=jnp.float32).astype(jnp.bfloat16)
    act_grad = jnp.dot(route_grad, weight_down, preferred_element_type=jnp.float32)
    pre_grad = jnp.concatenate([act_grad * up_part * sigmoid_gate * (1.0 + gate_part * (1.0 - sigmoid_gate)), act_grad * (gate_part * sigmoid_gate)], axis=1).astype(jnp.bfloat16)
    input_rows = lax.dot_general(pre_grad, weight_in, (((1,), (1,)), ((), ())), preferred_element_type=jnp.float32).astype(jnp.bfloat16)
    grad_in = lax.dot_general(row_inputs, pre_grad, (((0,), (0,)), ((), ())), preferred_element_type=jnp.float32)
    grad_down = lax.dot_general(route_grad, activation, (((0,), (0,)), ((), ())), preferred_element_type=jnp.float32)
    return (routed, input_rows, jnp.concatenate([grad_in, grad_down], axis=1))

def pick_rows(table, index):
    return table[index]

def reference(tokens, route_gates, expert_ids, owner_now, owner_next, out_grad, expert_weights, first_moment, second_moment):
    experts = N_EXPERT
    groups = N_DP
    capacity = CAP
    slot_total = experts * capacity
    model_width = tokens.shape[1]
    tok_groups = tokens.reshape(groups, experts, TOK_DEV, model_width)
    grad_groups = out_grad.reshape(groups, experts, TOK_DEV, model_width)
    gate_groups = route_gates.reshape(groups, experts, TOK_DEV, ROUTES)
    id_groups = expert_ids.reshape(groups, experts, TOK_DEV, ROUTES)

    def device_slots(ids_block):
        return route_slots(ids_block, owner_now, capacity)

    def device_rows(dest_block, gate_block):
        return slot_rows(dest_block, gate_block, slot_total)

    def one_slot(inputs):
        row_inputs, route_grad, weights = inputs
        return expert_pass(row_inputs.reshape(slot_total, model_width), route_grad.reshape(slot_total, model_width), weights)

    def one_group(grad_total, group_data):
        tok_block, grad_block, gate_block, ids_block = group_data
        destination = jax.vmap(device_slots)(ids_block)
        row_token, row_live, row_gate = jax.vmap(device_rows)(destination, gate_block)
        sent_rows = jnp.where(row_live[:, :, None], jax.vmap(pick_rows)(tok_block, row_token), 0)
        scaled = jax.vmap(pick_rows)(grad_block, row_token).astype(jnp.float32) * row_gate[:, :, None]
        route_grad = jnp.where(row_live[:, :, None], scaled, 0.0).astype(jnp.bfloat16)
        sent_rows = jnp.swapaxes(sent_rows.reshape(experts, experts, capacity, model_width), 0, 1)
        route_grad = jnp.swapaxes(route_grad.reshape(experts, experts, capacity, model_width), 0, 1)
        routed, input_rows, grad_part = lax.map(one_slot, (sent_rows, route_grad, expert_weights))
        returned_out = jnp.swapaxes(routed.reshape(experts, experts, capacity, model_width), 0, 1).reshape(experts, slot_total, model_width)
        returned_dx = jnp.swapaxes(input_rows.reshape(experts, experts, capacity, model_width), 0, 1).reshape(experts, slot_total, model_width)
        picked = jax.vmap(pick_rows)(returned_out, destination).astype(jnp.float32)
        moe_block = lax.optimization_barrier(jnp.sum(gate_block[..., None] * picked, axis=2)).astype(jnp.bfloat16)
        gate_block_grad = lax.optimization_barrier(jnp.sum(picked * grad_block.astype(jnp.float32)[:, :, None, :], axis=3))
        dx_block = lax.optimization_barrier(jnp.sum(jax.vmap(pick_rows)(returned_dx, destination).astype(jnp.float32), axis=2)).astype(jnp.bfloat16)
        rounded = lax.optimization_barrier(grad_part.astype(jnp.bfloat16)).astype(jnp.float32)
        return (grad_total + rounded, (moe_block, dx_block, gate_block_grad))
    start = jnp.zeros((experts, model_width, 3 * HID), jnp.float32)
    weight_grad, outs = lax.scan(one_group, start, (tok_groups, grad_groups, gate_groups, id_groups))
    moe_out = outs[0].reshape(TOKENS, model_width)
    tokens_grad = outs[1].reshape(TOKENS, model_width)
    gate_grads = outs[2].reshape(TOKENS, ROUTES)
    first_new = beta_one * first_moment.astype(jnp.float32) + (1.0 - beta_one) * weight_grad
    second_new = beta_two * second_moment.astype(jnp.float32) + (1.0 - beta_two) * weight_grad * weight_grad
    weight_new = expert_weights.astype(jnp.float32) - learn_rate * first_new / (jnp.sqrt(second_new) + adam_eps)
    source = owner_sources(owner_now, owner_next)
    new_weights = weight_new[source].astype(jnp.bfloat16)
    new_first = first_new[source].astype(jnp.bfloat16)
    new_second = second_new[source].astype(jnp.bfloat16)
    return (moe_out, tokens_grad, gate_grads, new_weights, new_first, new_second)
```

```python
import functools

import jax
import jax.numpy as jnp
from jax import lax
from jax.experimental import pallas as pl
from jax.experimental.pallas import tpu as pltpu
from jax.sharding import PartitionSpec as P

MESH = pl.DeviceIdType.MESH
BF16 = jnp.bfloat16
F32 = jnp.float32

beta_one = 0.9
beta_two = 0.95
learn_rate = 0.003
adam_eps = 1e-08

SLOT = 16
WIDE, NARROW = 256, 128
CHUNKS = 2


def dot(a, b, dims):
    return lax.dot_general(a, b, (dims, ((), ())), preferred_element_type=F32)


def kernel(
    cfg,
    source,
    tokens,
    gates,
    ids,
    owner_next,
    out_grad,
    w_old,
    m_old,
    v_old,
    moe_out,
    tokens_grad,
    gate_grads,
    w_new,
    m_new,
    v_new,
    x_send,
    g_send,
    x_in,
    g_in,
    weights,
    gate_up,
    act,
    pre,
    ro_send,
    dx_send,
    ro_in,
    dx_in,
    sum_send,
    sum_in,
    part,
    place,
    place_gate,
    hop_w_a,
    hop_m_a,
    hop_v_a,
    hop_w_b,
    hop_m_b,
    hop_v_b,
    out_a,
    out_b,
    moments,
    a2a_s,
    a2a_r,
    hop1_s,
    hop1_r,
    hop2_s,
    hop2_r,
    ag_s,
    ag_r,
    rs_s,
    rs_r,
):
    groups, experts, xs, ys = cfg
    hop_a, hop_b = (hop_w_a, hop_m_a, hop_v_a), (hop_w_b, hop_m_b, hop_v_b)
    dp = lax.axis_index("dp")
    me = lax.axis_index("expert")
    tok, width = tokens.shape
    rows, cols = w_old.shape
    hid = cols // 3
    slots = experts * SLOT
    n_wide = cols // WIDE
    n_row = rows // SLOT
    n_right = groups // 2
    n_left = groups - 1 - n_right
    part_rows = rows // CHUNKS
    right = lax.rem(dp + 1, groups)
    left = lax.rem(dp + groups - 1, groups)
    my_x, my_y, my_c = me // (2 * ys), (me // 2) % ys, me % 2

    def peer(i):
        off = (i * 11) % experts
        px = (my_x + off // (2 * ys)) % xs
        py = (my_y + (off // 2) % ys) % ys
        return (px * ys + py) * 2 + (my_c + off) % 2

    def each_peer(low, high, body):
        def step(i, carry):
            body(peer(i))
            return carry

        lax.fori_loop(low, high, step, 0)

    def remote(src, dst, ssem, rsem, device):
        pltpu.make_async_remote_copy(
            src_ref=src,
            dst_ref=dst,
            send_sem=ssem,
            recv_sem=rsem,
            device_id=device,
            device_id_type=MESH,
        ).start()

    def await_bytes(ref, sem):
        pltpu.make_async_copy(ref, ref, sem).wait()

    barrier = pltpu.get_barrier_semaphore()
    each_peer(
        1,
        experts,
        lambda d: pl.semaphore_signal(
            barrier, inc=1, device_id=(dp, d), device_id_type=MESH
        ),
    )
    for z in (left, right):
        pl.semaphore_signal(barrier, inc=1, device_id=(z, me), device_id_type=MESH)
    pl.semaphore_wait(barrier, experts + 1)

    def piece(ref, relay, base=0):
        return ref.at[
            pl.ds(pl.multiple_of(base + (relay // n_wide) * SLOT, SLOT), SLOT),
            pl.ds(pl.multiple_of((relay % n_wide) * WIDE, WIDE), WIDE),
        ]

    def rest(ref, relay, base=0):
        return ref.at[
            pl.ds(pl.multiple_of(base + (relay // n_wide) * SLOT, SLOT), SLOT),
            pl.ds(n_wide * WIDE, NARROW),
        ]

    def hop_one(a, ref):
        chosen = a % n_wide

        def one(d):
            remote(piece(ref, d), hop_a[a].at[me], hop1_s.at[a, 0], hop1_r.at[a, 0], (dp, d))

            @pl.when(d % n_wide == chosen)
            def _():
                remote(rest(ref, d), hop_b[a].at[me], hop1_s.at[a, 1], hop1_r.at[a, 1], (dp, d))

        each_peer(1, experts, one)
        hop_a[a][me] = piece(ref, me)[...]

        @pl.when(me % n_wide == chosen)
        def _():
            hop_b[a][me] = rest(ref, me)[...]

    def hop_two(a, ref, base):
        chosen = a % n_wide
        await_bytes(hop_a[a].at[pl.ds(0, experts - 1)], hop1_r.at[a, 0])

        def pick_a(s, carry):
            out_a[a, s] = hop_a[a][source[s]]
            return carry

        lax.fori_loop(0, experts, pick_a, 0)
        each_peer(
            1,
            experts,
            lambda d: remote(
                out_a.at[a, d], piece(ref, me, base), hop2_s.at[a, 0], hop2_r.at[a, 0], (dp, d)
            ),
        )
        piece(ref, me, base)[...] = out_a[a, me]

        @pl.when(me % n_wide == chosen)
        def _():
            await_bytes(hop_b[a].at[pl.ds(0, experts - 1)], hop1_r.at[a, 1])

            def pick_b(s, carry):
                out_b[a, s] = hop_b[a][source[s]]
                return carry

            lax.fori_loop(0, experts, pick_b, 0)
            each_peer(
                1,
                experts,
                lambda d: remote(
                    out_b.at[a, d], rest(ref, me, base), hop2_s.at[a, 1], hop2_r.at[a, 1], (dp, d)
                ),
            )
            rest(ref, me, base)[...] = out_b[a, me]

    def narrow_wait(a, sem):
        chosen = a % n_wide

        @pl.when(me % n_wide == chosen)
        def _():
            await_bytes(hop_b[a].at[pl.ds(0, n_row - 1)], sem)

        @pl.when(me % n_wide != chosen)
        def _():
            await_bytes(hop_b[a].at[pl.ds(0, n_row)], sem)

    def arrived(a):
        await_bytes(hop_a[a].at[pl.ds(0, experts - 1)], hop2_r.at[a, 0])
        narrow_wait(a, hop2_r.at[a, 1])

    def hops_sent(a):
        await_bytes(hop_a[a].at[pl.ds(0, experts - 1)], hop1_s.at[a, 0])
        narrow_wait(a, hop1_s.at[a, 1])
        await_bytes(hop_a[a].at[pl.ds(0, experts - 1)], hop2_s.at[a, 0])

        @pl.when(me % n_wide == a % n_wide)
        def _():
            await_bytes(hop_b[a].at[pl.ds(0, experts - 1)], hop2_s.at[a, 1])

    def zone(z, ch=0, size=None):
        start = ((z + groups) % groups) * rows + ch * part_rows
        return pl.ds(pl.multiple_of(start, part_rows), size or rows)

    hop_one(0, w_old)

    lane = lax.broadcasted_iota(jnp.int32, (tok, experts), 1)
    hits = [(ids[:, r : r + 1] == lane).astype(F32) for r in range(3)]
    before = lax.broadcasted_iota(jnp.int32, (tok, tok), 1) < lax.broadcasted_iota(
        jnp.int32, (tok, tok), 0
    )
    position = dot(
        before.astype(F32).astype(BF16),
        (hits[0] + hits[1] + hits[2]).astype(BF16),
        ((1,), (0,)),
    )
    row_at = owner_next[...].astype(F32) * SLOT + position
    target = [
        jnp.sum(h * row_at, axis=1, keepdims=True).astype(jnp.int32) for h in hits
    ]
    slot_lane = lax.broadcasted_iota(jnp.int32, (tok, slots), 1)
    spread = jnp.zeros((tok, slots), F32)
    weighted = jnp.zeros((tok, slots), F32)
    for r in range(3):
        here = slot_lane == target[r]
        spread = spread + here.astype(F32)
        weighted = weighted + jnp.where(here, gates[:, r : r + 1], 0.0)
    place[...] = spread
    place_gate[...] = weighted
    rows_of = spread.T.astype(BF16)
    gate_of = jnp.sum(weighted.T, axis=1, keepdims=True)

    block = min(256, width)

    def gather(c, carry):
        at = pl.ds(pl.multiple_of(c * block, block), block)
        x_send[:, at] = dot(rows_of, tokens[:, at], ((1,), (0,))).astype(BF16)
        g_send[:, at] = (dot(rows_of, out_grad[:, at], ((1,), (0,))) * gate_of).astype(BF16)
        return carry

    lax.fori_loop(0, width // block, gather, 0)

    hop_two(0, weights, dp * rows)

    def send_rows(n, src, dst):
        def one(d):
            remote(
                src.at[pl.ds(pl.multiple_of(d * SLOT, SLOT), SLOT)],
                dst.at[pl.ds(pl.multiple_of(me * SLOT, SLOT), SLOT)],
                a2a_s.at[n],
                a2a_r.at[n],
                (dp, d),
            )

        return one

    mine = pl.ds(pl.multiple_of(me * SLOT, SLOT), SLOT)

    def dispatch(low, high):
        def both(d):
            send_rows(0, x_send, x_in)(d)
            send_rows(1, g_send, g_in)(d)

        each_peer(low, high, both)

    def rows_arrived(n, ref):
        await_bytes(ref.at[pl.ds(0, (experts - 1) * SLOT)], a2a_r.at[n])

    def share(total, steps, k):
        per = -(-total // steps)
        return 1 + jnp.minimum(k * per, total), 1 + jnp.minimum((k + 1) * per, total)

    others = experts - 1
    dispatch(*share(others, n_right, 0))
    x_in[mine, :] = x_send[mine, :]
    g_in[mine, :] = g_send[mine, :]

    def gather_copy(way, k, ch):
        at = zone(dp - k if way == 0 else dp + k, ch, part_rows)
        remote(
            weights.at[at],
            weights.at[at],
            ag_s.at[way, k, ch],
            ag_r.at[way, k, ch],
            (right if way == 0 else left, me),
        )

    arrived(0)
    for ch in range(CHUNKS):
        gather_copy(0, 0, ch)
        if n_left:
            gather_copy(1, 0, ch)

    def gather_step(k, carry):
        for ch in range(CHUNKS):
            for way, count in ((0, n_right), (1, n_left)):

                @pl.when(k < count)
                def _():
                    z = dp - k - 1 if way == 0 else dp + k + 1
                    await_bytes(weights.at[zone(z, ch, part_rows)], ag_r.at[way, k, ch])

                @pl.when(k + 1 < count)
                def _():
                    gather_copy(way, k + 1, ch)

        @pl.when(k + 1 < n_right)
        def _():
            dispatch(*share(others, n_right, k + 1))

        return carry

    lax.fori_loop(0, n_right, gather_step, 0)

    hop_one(1, m_old)
    hop_one(2, v_old)

    rows_arrived(0, x_in)
    rows_arrived(1, g_in)
    for c in range(0, 3 * hid, min(256, hid)):
        n = min(256, hid)
        if c < 2 * hid:
            gate_up[:, c : c + n] = dot(x_in[...], weights[:, c : c + n], ((1,), (0,)))
    for c in range(0, hid, 128):
        gate_up[:, 2 * hid + c : 2 * hid + c + 128] = dot(
            g_in[...], weights[:, 2 * hid + c : 2 * hid + c + 128], ((1,), (0,))
        )

    height = min(64, slots)

    def hidden(c, carry):
        at = pl.ds(pl.multiple_of(c * height, height), height)
        gate = gate_up[at, 0:hid]
        up = gate_up[at, hid : 2 * hid]
        grad = gate_up[at, 2 * hid : 3 * hid]
        sig = jax.nn.sigmoid(gate)
        act[at, :] = (gate * sig * up).astype(BF16)
        pre[at, 0:hid] = (grad * up * sig * (1.0 + gate * (1.0 - sig))).astype(BF16)
        pre[at, hid : 2 * hid] = (grad * (gate * sig)).astype(BF16)
        return carry

    lax.fori_loop(0, slots // height, hidden, 0)

    def partial(z, n):
        at = zone(z)
        part[n, :, 0 : 2 * hid] = dot(x_in[:, at], pre[...], ((0,), (0,)))
        part[n, :, 2 * hid : 3 * hid] = dot(g_in[:, at], act[...], ((0,), (0,)))

    def sum_copy(way, k, ch):
        at = pl.ds(ch * part_rows, part_rows)
        remote(
            sum_send.at[way, k, at],
            sum_in.at[way, k, at],
            rs_s.at[way, k, ch],
            rs_r.at[way, k, ch],
            (right if way == 0 else left, me),
        )

    def sum_arrived(way, k, ch):
        at = pl.ds(ch * part_rows, part_rows)
        await_bytes(sum_in.at[way, k, at], rs_r.at[way, k, ch])

    for way, count, z in ((0, n_right, dp + n_right), (1, n_left, dp - n_left)):
        if count:
            partial(z, way)
            sum_send[way, 0] = part[way].astype(BF16)
            for ch in range(CHUNKS):
                sum_copy(way, 0, ch)

    hop_two(1, moments.at[0], 0)
    hop_two(2, moments.at[1], 0)

    def route_out(c, carry):
        at = pl.ds(pl.multiple_of(c * block, block), block)
        ro_send[:, at] = dot(act[...], weights[at, 2 * hid : 3 * hid], ((1,), (1,))).astype(BF16)
        dx_send[:, at] = dot(pre[...], weights[at, 0 : 2 * hid], ((1,), (1,))).astype(BF16)
        return carry

    lax.fori_loop(0, width // block, route_out, 0)

    def give_back(low, high):
        def both(d):
            send_rows(2, ro_send, ro_in)(d)
            send_rows(3, dx_send, dx_in)(d)

        each_peer(low, high, both)

    give_back(*share(others, 4, 0))
    ro_in[mine, :] = ro_send[mine, :]
    dx_in[mine, :] = dx_send[mine, :]

    def sum_step(k, carry):
        partial(dp + n_right - k, 0)

        @pl.when(k < n_left)
        def _():
            partial(dp - n_left + k, 1)

        for ch in range(CHUNKS):
            at = pl.ds(ch * part_rows, part_rows)
            for way, count in ((0, n_right), (1, n_left)):

                @pl.when(k < count)
                def _():
                    sum_arrived(way, k - 1, ch)
                    sum_send[way, k, at] = (
                        part[way, at] + sum_in[way, k - 1, at].astype(F32)
                    ).astype(BF16)
                    sum_copy(way, k, ch)

        @pl.when(k < 4)
        def _():
            give_back(*share(others, 4, k))

        return carry

    lax.fori_loop(1, n_right, sum_step, 0)
    for k in range(n_right, 4):
        give_back(*share(others, 4, k))
    partial(dp, 0)

    rows_arrived(2, ro_in)
    gate_high = place_gate[...].astype(BF16)
    gate_low = (place_gate[...] - gate_high.astype(F32)).astype(BF16)

    def combine(c, total):
        at = pl.ds(pl.multiple_of(c * block, block), block)
        rows_here = ro_in[:, at]
        moe_out[:, at] = (
            dot(gate_high, rows_here, ((1,), (0,))) + dot(gate_low, rows_here, ((1,), (0,)))
        ).astype(BF16)
        return total + dot(out_grad[:, at], rows_here, ((1,), (1,)))

    products = lax.fori_loop(0, width // block, combine, jnp.zeros((tok, slots), F32))
    for r in range(3):
        gate_grads[:, r : r + 1] = jnp.sum(
            jnp.where(slot_lane == target[r], products, 0.0), axis=1, keepdims=True
        )
    rows_arrived(3, dx_in)
    spread_low = place[...].astype(BF16)

    def combine_dx(c, carry):
        at = pl.ds(pl.multiple_of(c * block, block), block)
        tokens_grad[:, at] = dot(spread_low, dx_in[:, at], ((1,), (0,))).astype(BF16)
        return carry

    lax.fori_loop(0, width // block, combine_dx, 0)

    arrived(1)
    arrived(2)
    for ch in range(CHUNKS):
        sum_arrived(0, n_right - 1, ch)
        if n_left:
            sum_arrived(1, n_left - 1, ch)
    w_base = dp * rows

    def adam(c, carry):
        at = pl.ds(pl.multiple_of(c * SLOT, SLOT), SLOT)
        grad = part[0, at] + sum_in[0, n_right - 1, at].astype(F32)
        if n_left:
            grad = grad + sum_in[1, n_left - 1, at].astype(F32)
        first = beta_one * moments[0, at].astype(F32) + (1.0 - beta_one) * grad
        second = beta_two * moments[1, at].astype(F32) + (1.0 - beta_two) * grad * grad
        old = weights[pl.ds(pl.multiple_of(w_base + c * SLOT, SLOT), SLOT), :].astype(F32)
        w_new[at, :] = (old - learn_rate * first / (jnp.sqrt(second) + adam_eps)).astype(BF16)
        m_new[at, :] = first.astype(BF16)
        v_new[at, :] = second.astype(BF16)
        return carry

    lax.fori_loop(0, rows // SLOT, adam, 0)

    for n, ref in enumerate((x_send, g_send, ro_send, dx_send)):
        await_bytes(ref.at[pl.ds(0, others * SLOT)], a2a_s.at[n])
    for a in range(3):
        hops_sent(a)
    for way, count in ((0, n_right), (1, n_left)):

        def left_here(k, carry):
            for ch in range(CHUNKS):
                at = pl.ds(ch * part_rows, part_rows)
                await_bytes(sum_send.at[way, k, at], ag_s.at[way, k, ch])
                await_bytes(sum_send.at[way, k, at], rs_s.at[way, k, ch])
            return carry

        lax.fori_loop(0, count, left_here, 0)


def shards(
    grid,
    tokens,
    route_gates,
    expert_ids,
    owner_now,
    owner_next,
    out_grad,
    expert_weights,
    first_moment,
    second_moment,
):
    groups, experts = lax.axis_size("dp"), lax.axis_size("expert")
    tok, width = tokens.shape
    _, rows, cols = expert_weights.shape
    hid = cols // 3
    slots = experts * SLOT
    n_right = groups // 2
    matches = owner_next[None, :] == jnp.arange(experts, dtype=jnp.int32)[:, None]
    source = jnp.sum(jnp.where(matches, owner_now[None, :], 0), axis=1)
    vmem = pl.BlockSpec(memory_space=pltpu.VMEM)
    dma = pltpu.SemaphoreType.DMA
    state = jax.ShapeDtypeStruct((rows, cols), BF16)
    result = pl.pallas_call(
        functools.partial(kernel, (groups, experts, *grid)),
        out_shape=(
            jax.ShapeDtypeStruct((tok, width), BF16),
            jax.ShapeDtypeStruct((tok, width), BF16),
            jax.ShapeDtypeStruct(route_gates.shape, F32),
            state,
            state,
            state,
        ),
        in_specs=[pl.BlockSpec(memory_space=pltpu.SMEM)] + [vmem] * 8,
        out_specs=(vmem,) * 6,
        scratch_shapes=[
            pltpu.VMEM((slots, width), BF16),
            pltpu.VMEM((slots, width), BF16),
            pltpu.VMEM((slots, width), BF16),
            pltpu.VMEM((slots, width), BF16),
            pltpu.VMEM((width, cols), BF16),
            pltpu.VMEM((slots, cols), F32),
            pltpu.VMEM((slots, hid), BF16),
            pltpu.VMEM((slots, 2 * hid), BF16),
            pltpu.VMEM((slots, width), BF16),
            pltpu.VMEM((slots, width), BF16),
            pltpu.VMEM((slots, width), BF16),
            pltpu.VMEM((slots, width), BF16),
            pltpu.VMEM((2, n_right, rows, cols), BF16),
            pltpu.VMEM((2, n_right, rows, cols), BF16),
            pltpu.VMEM((2, rows, cols), F32),
            pltpu.VMEM((tok, slots), F32),
            pltpu.VMEM((tok, slots), F32),
            *[pltpu.VMEM((experts, SLOT, WIDE), BF16)] * 3,
            *[pltpu.VMEM((experts, SLOT, NARROW), BF16)] * 3,
            pltpu.VMEM((3, experts, SLOT, WIDE), BF16),
            pltpu.VMEM((3, experts, SLOT, NARROW), BF16),
            pltpu.VMEM((2, rows, cols), BF16),
            dma((4,)),
            dma((4,)),
            dma((3, 2)),
            dma((3, 2)),
            dma((3, 2)),
            dma((3, 2)),
            dma((2, n_right, CHUNKS)),
            dma((2, n_right, CHUNKS)),
            dma((2, n_right, CHUNKS)),
            dma((2, n_right, CHUNKS)),
        ],
        compiler_params=pltpu.CompilerParams(
            collective_id=0, has_side_effects=True, vmem_limit_bytes=60 * 2**20
        ),
        name="moe_step",
    )(
        source,
        tokens,
        route_gates,
        expert_ids,
        owner_next[None, :],
        out_grad,
        expert_weights[0],
        first_moment[0],
        second_moment[0],
    )
    moe_out, tokens_grad, gate_grads, w_new, m_new, v_new = result
    return (moe_out, tokens_grad, gate_grads, w_new[None], m_new[None], v_new[None])


def solution(mesh):
    pairs = mesh.shape["expert"] // 2
    ys = 1
    while ys * ys * 4 <= pairs:
        ys *= 2
    by_token = P(("dp", "expert"), None)
    by_state = P("expert", "dp", None)
    return jax.shard_map(
        functools.partial(shards, (pairs // ys, ys)),
        mesh=mesh,
        in_specs=(by_token,) * 3 + (P(), P()) + (by_token,) + (by_state,) * 3,
        out_specs=(by_token,) * 3 + (by_state,) * 3,
        check_vma=False,
    )
```

```python
import functools

import jax
import jax.numpy as jnp
from jax import lax
from jax.experimental import pallas as pl
from jax.experimental.pallas import tpu as pltpu
from jax.sharding import PartitionSpec as P

MESH = pl.DeviceIdType.MESH
BF16 = jnp.bfloat16
F32 = jnp.float32

beta_one = 0.9
beta_two = 0.95
learn_rate = 0.003
adam_eps = 1e-08

SLOT = 16
WIDE, NARROW = 256, 128
X_STEPS, G_STEPS = 2, 4
CHUNKS = 2


def dot(a, b, dims):
    return lax.dot_general(a, b, (dims, ((), ())), preferred_element_type=F32)


def kernel(
    cfg,
    source,
    tokens,
    gates,
    ids,
    owner_next,
    out_grad,
    w_old,
    m_old,
    v_old,
    moe_out,
    tokens_grad,
    gate_grads,
    w_new,
    m_new,
    v_new,
    x_send,
    g_send,
    x_in,
    g_in,
    weights,
    gate_up,
    act,
    pre,
    ro_send,
    dx_send,
    ro_in,
    dx_in,
    sum_send,
    sum_in,
    part,
    place,
    place_t,
    high_t,
    low_t,
    gate_of,
    hop_w_a,
    hop_w_b,
    out_w_a,
    out_w_b,
    hop_m_a,
    hop_m_b,
    out_m_a,
    out_m_b,
    moments_old,
    moments,
    load_s,
    a2a_s,
    a2a_r,
    hop1_s,
    hop1_r,
    hop2_s,
    hop2_r,
    ag_s,
    ag_r,
    rs_s,
    rs_r,
):
    groups, experts, xs, ys = cfg
    hop_a, hop_b = (hop_w_a, hop_m_a), (hop_w_b, hop_m_b)
    out_a, out_b = (out_w_a, out_m_a), (out_w_b, out_m_b)
    dp = lax.axis_index("dp")
    me = lax.axis_index("expert")
    tok, width = tokens.shape
    rows, cols = w_old.shape
    hid = cols // 3
    slots = experts * SLOT
    others = experts - 1
    n_wide = cols // WIDE
    n_row = rows // SLOT
    half = groups // 2
    part_rows = rows // CHUNKS
    right = lax.rem(dp + 1, groups)
    left = lax.rem(dp + groups - 1, groups)
    y_bits = ys.bit_length()
    low_bits = (1 << y_bits) - 1

    def peer(i):
        off = (i * 11) & (experts - 1)
        x_part = ((me >> y_bits) + (off >> y_bits)) & (xs - 1)
        y_part = ((me & low_bits & ~1) + (off & low_bits & ~1)) & low_bits
        return (x_part << y_bits) | y_part | ((me ^ off) & 1)

    def each_peer(low, high, body):
        def step(i, carry):
            body(peer(i))
            return carry

        lax.fori_loop(low, high, step, 0)

    def remote(src, dst, ssem, rsem, device):
        pltpu.make_async_remote_copy(
            src_ref=src,
            dst_ref=dst,
            send_sem=ssem,
            recv_sem=rsem,
            device_id=device,
            device_id_type=MESH,
        ).start()

    def await_bytes(ref, sem):
        pltpu.make_async_copy(ref, ref, sem).wait()

    loads = [
        pltpu.make_async_copy(ref, moments_old.at[n], load_s.at[n])
        for n, ref in enumerate((m_old, v_old))
    ]
    for load in loads:
        load.start()

    barrier = pltpu.get_barrier_semaphore()
    each_peer(
        1,
        experts,
        lambda d: pl.semaphore_signal(
            barrier, inc=1, device_id=(dp, d), device_id_type=MESH
        ),
    )
    for z in (left, right):
        pl.semaphore_signal(barrier, inc=1, device_id=(z, me), device_id_type=MESH)
    pl.semaphore_wait(barrier, experts + 1)

    shift = n_wide.bit_length() - 1

    def piece(ref, lead, relay, base=0):
        return ref.at[
            (
                *lead,
                pl.ds(pl.multiple_of(base + (relay >> shift) * SLOT, SLOT), SLOT),
                pl.ds(pl.multiple_of((relay & (n_wide - 1)) * WIDE, WIDE), WIDE),
            )
        ]

    def rest(ref, lead, relay, base=0):
        return ref.at[
            (
                *lead,
                pl.ds(pl.multiple_of(base + (relay >> shift) * SLOT, SLOT), SLOT),
                pl.ds(n_wide * WIDE, NARROW),
            )
        ]

    def narrow(a, device):
        return (device & (n_wide - 1)) == a % n_wide

    leads = ((), (slice(None),))

    def hop_one(a, ref):
        def one(d):
            remote(
                piece(ref, leads[a], d), hop_a[a].at[me], hop1_s.at[a, 0], hop1_r.at[a, 0], (dp, d)
            )

            @pl.when(narrow(a, d))
            def _():
                remote(
                    rest(ref, leads[a], d), hop_b[a].at[me], hop1_s.at[a, 1], hop1_r.at[a, 1], (dp, d)
                )

        each_peer(1, experts, one)
        hop_a[a][me] = piece(ref, leads[a], me)[...]

        @pl.when(narrow(a, me))
        def _():
            hop_b[a][me] = rest(ref, leads[a], me)[...]

    def hop_two(a, ref, base):
        def pass_on(n, hop, out, part_of):
            await_bytes(hop.at[pl.ds(0, others)], hop1_r.at[a, n])

            def pick(s, carry):
                out[s] = hop[source[s]]
                return carry

            lax.fori_loop(0, experts, pick, 0)
            each_peer(
                1,
                experts,
                lambda d: remote(
                    out.at[d],
                    part_of(ref, leads[a], me, base),
                    hop2_s.at[a, n],
                    hop2_r.at[a, n],
                    (dp, d),
                ),
            )
            part_of(ref, leads[a], me, base)[...] = out[me]

        pass_on(0, hop_a[a], out_a[a], piece)

        @pl.when(narrow(a, me))
        def _():
            pass_on(1, hop_b[a], out_b[a], rest)

    def narrow_wait(a, sem):
        @pl.when(narrow(a, me))
        def _():
            await_bytes(hop_b[a].at[pl.ds(0, n_row - 1)], sem)

        @pl.when(jnp.logical_not(narrow(a, me)))
        def _():
            await_bytes(hop_b[a].at[pl.ds(0, n_row)], sem)

    def arrived(a):
        await_bytes(hop_a[a].at[pl.ds(0, others)], hop2_r.at[a, 0])
        narrow_wait(a, hop2_r.at[a, 1])

    def hops_sent(a):
        await_bytes(hop_a[a].at[pl.ds(0, others)], hop1_s.at[a, 0])
        narrow_wait(a, hop1_s.at[a, 1])
        await_bytes(hop_a[a].at[pl.ds(0, others)], hop2_s.at[a, 0])

        @pl.when(narrow(a, me))
        def _():
            await_bytes(hop_b[a].at[pl.ds(0, others)], hop2_s.at[a, 1])

    def zone(z, ch=0, size=None):
        start = ((z + groups) & (groups - 1)) * rows + ch * part_rows
        return pl.ds(pl.multiple_of(start, part_rows), size or rows)

    def on_far(way, ch):
        return (ch < CHUNKS // 2) == (way == 0)

    hop_one(0, w_old)

    expert_row = lax.broadcasted_iota(jnp.int32, (experts, tok), 0)
    hits = [(ids[r : r + 1, :] == expert_row).astype(F32) for r in range(3)]
    before = lax.broadcasted_iota(jnp.int32, (tok, tok), 0) < lax.broadcasted_iota(
        jnp.int32, (tok, tok), 1
    )
    position = dot(
        (hits[0] + hits[1] + hits[2]).astype(BF16),
        before.astype(F32).astype(BF16),
        ((1,), (0,)),
    )
    diagonal = lax.broadcasted_iota(jnp.int32, (experts, experts), 0) == lax.broadcasted_iota(
        jnp.int32, (experts, experts), 1
    )
    holder = jnp.sum(
        jnp.where(diagonal, owner_next[...].astype(F32), 0.0), axis=1, keepdims=True
    )
    row_at = holder * SLOT + position
    target = [
        jnp.sum(h * row_at, axis=0, keepdims=True).astype(jnp.int32) for h in hits
    ]
    slot_row = lax.broadcasted_iota(jnp.int32, (slots, tok), 0)
    spread = jnp.zeros((slots, tok), F32)
    weighted = jnp.zeros((slots, tok), F32)
    for r in range(3):
        here = slot_row == target[r]
        spread = spread + here.astype(F32)
        weighted = weighted + jnp.where(here, gates[r : r + 1, :], 0.0)
    place[...] = spread.astype(BF16)
    block = min(256, width)

    def gather_x(c, carry):
        at = pl.ds(pl.multiple_of(c * block, block), block)
        x_send[:, at] = dot(place[...], tokens[:, at], ((1,), (0,))).astype(BF16)
        return carry

    lax.fori_loop(0, width // block, gather_x, 0)

    hop_two(0, weights, dp * rows)

    mine = pl.ds(pl.multiple_of(me * SLOT, SLOT), SLOT)

    def send_rows(n, src, dst, low, high):
        each_peer(
            low,
            high,
            lambda d: remote(
                src.at[pl.ds(pl.multiple_of(d * SLOT, SLOT), SLOT)],
                dst.at[mine],
                a2a_s.at[n],
                a2a_r.at[n],
                (dp, d),
            ),
        )

    def rows_arrived(n, ref):
        await_bytes(ref.at[pl.ds(0, others * SLOT)], a2a_r.at[n])

    def share(steps, k):
        per = -(-others // steps)
        return 1 + jnp.minimum(k * per, others), 1 + jnp.minimum((k + 1) * per, others)

    send_rows(0, x_send, x_in, *share(X_STEPS, 0))
    x_in[mine, :] = x_send[mine, :]

    def gather_copy(way, k, ch):
        at = zone(dp - k if way == 0 else dp + k, ch, part_rows)
        remote(
            weights.at[at],
            weights.at[at],
            ag_s.at[way, k, ch],
            ag_r.at[way, k, ch],
            (right if way == 0 else left, me),
        )

    def gathered(way, k, ch):
        z = dp - k - 1 if way == 0 else dp + k + 1
        await_bytes(weights.at[zone(z, ch, part_rows)], ag_r.at[way, k, ch])

    arrived(0)
    for ch in range(CHUNKS):
        for way in (0, 1):
            gather_copy(way, 0, ch)

    for k in range(1, X_STEPS):
        send_rows(0, x_send, x_in, *share(X_STEPS, k))

    gate_of[...] = jnp.sum(weighted, axis=1, keepdims=True)

    def gather_g(c, carry):
        at = pl.ds(pl.multiple_of(c * block, block), block)
        g_send[:, at] = (
            dot(place[...], out_grad[:, at], ((1,), (0,))) * gate_of[...]
        ).astype(BF16)
        return carry

    lax.fori_loop(0, width // block, gather_g, 0)
    g_in[mine, :] = g_send[mine, :]

    def gather_step(k, carry):
        for ch in range(CHUNKS):
            for way in (0, 1):
                gathered(way, k, ch)

                if on_far(way, ch):
                    gather_copy(way, k + 1, ch)
                else:

                    @pl.when(k + 1 < half - 1)
                    def _():
                        gather_copy(way, k + 1, ch)

        @pl.when(k < G_STEPS)
        def _():
            send_rows(1, g_send, g_in, *share(G_STEPS, k))

        return carry

    lax.fori_loop(0, half - 1, gather_step, 0)
    for k in range(half - 1, G_STEPS):
        send_rows(1, g_send, g_in, *share(G_STEPS, k))

    for load in loads:
        load.wait()
    hop_one(1, moments_old)

    weighted_t = weighted.T
    high = weighted_t.astype(BF16)
    high_t[...] = high
    low_t[...] = (weighted_t - high.astype(F32)).astype(BF16)
    place_t[...] = spread.T.astype(BF16)

    def hidden_sums(rows_here, base, zs, first):
        step = min(256, hid) if base == 0 else hid
        for c in range(base, 2 * hid if base == 0 else 3 * hid, step):
            total = None
            for z in zs:
                term = dot(
                    jnp.concatenate([rows_here[:, zone(i)] for i in z], axis=1),
                    jnp.concatenate([weights[zone(i), c : c + step] for i in z], axis=0),
                    ((1,), (0,)),
                )
                total = term if total is None else total + term
            gate_up[:, c : c + step] = total if first else gate_up[:, c : c + step] + total

    near = [dp + half + 1 + n for n in range(groups - 1)]
    near = [near[n : n + 2] for n in range(0, groups - 1, 2)]
    rows_arrived(0, x_in)
    hidden_sums(x_in, 0, near, True)
    rows_arrived(1, g_in)
    hidden_sums(g_in, 2 * hid, near, True)
    for ch in range(CHUNKS):
        gathered(0 if on_far(0, ch) else 1, half - 1, ch)
    hidden_sums(x_in, 0, [[dp + half]], False)
    hidden_sums(g_in, 2 * hid, [[dp + half]], False)

    height = min(64, slots)

    def hidden(c, carry):
        at = pl.ds(pl.multiple_of(c * height, height), height)
        gate = gate_up[at, 0:hid]
        up = gate_up[at, hid : 2 * hid]
        grad = gate_up[at, 2 * hid : 3 * hid]
        sig = jax.nn.sigmoid(gate)
        act[at, :] = (gate * sig * up).astype(BF16)
        pre[at, 0:hid] = (grad * up * sig * (1.0 + gate * (1.0 - sig))).astype(BF16)
        pre[at, hid : 2 * hid] = (grad * (gate * sig)).astype(BF16)
        return carry

    lax.fori_loop(0, slots // height, hidden, 0)

    def partial(z, n):
        at = zone(z)
        part[n, :, 0 : 2 * hid] = dot(x_in[:, at], pre[...], ((0,), (0,)))
        part[n, :, 2 * hid : 3 * hid] = dot(g_in[:, at], act[...], ((0,), (0,)))

    def sum_copy(way, k, ch):
        at = pl.ds(ch * part_rows, part_rows)
        remote(
            sum_send.at[way, k, at],
            sum_in.at[way, k, at],
            rs_s.at[way, k, ch],
            rs_r.at[way, k, ch],
            (right if way == 0 else left, me),
        )

    def sum_arrived(way, k, ch):
        at = pl.ds(ch * part_rows, part_rows)
        await_bytes(sum_in.at[way, k, at], rs_r.at[way, k, ch])

    partial(dp + half, 0)
    for ch in range(CHUNKS):
        way = 0 if on_far(0, ch) else 1
        at = pl.ds(ch * part_rows, part_rows)
        sum_send[way, 0, at] = part[0, at].astype(BF16)
        sum_copy(way, 0, ch)

    def route_out(c, carry):
        at = pl.ds(pl.multiple_of(c * block, block), block)
        ro_send[:, at] = dot(act[...], weights[at, 2 * hid : 3 * hid], ((1,), (1,))).astype(BF16)
        return carry

    lax.fori_loop(0, width // block, route_out, 0)
    send_rows(2, ro_send, ro_in, 1, experts)
    ro_in[mine, :] = ro_send[mine, :]

    def sum_step(k, carry):
        partial(dp + half - k, 0)
        partial(dp - half + k, 1)

        for ch in range(CHUNKS):
            at = pl.ds(ch * part_rows, part_rows)
            for way in (0, 1):

                def add():
                    sum_arrived(way, k - 1, ch)
                    sum_send[way, k, at] = (
                        part[way, at] + sum_in[way, k - 1, at].astype(F32)
                    ).astype(BF16)

                if on_far(way, ch):
                    add()
                else:
                    pl.when(k > 1)(add)

                    @pl.when(k == 1)
                    def _():
                        sum_send[way, k, at] = part[way, at].astype(BF16)

                sum_copy(way, k, ch)
        return carry

    def give_dx():
        def dx_out(c, carry):
            at = pl.ds(pl.multiple_of(c * block, block), block)
            dx_send[:, at] = dot(pre[...], weights[at, 0 : 2 * hid], ((1,), (1,))).astype(BF16)
            return carry

        lax.fori_loop(0, width // block, dx_out, 0)
        send_rows(3, dx_send, dx_in, 1, experts)
        dx_in[mine, :] = dx_send[mine, :]
        hop_two(1, moments, 0)

    lax.fori_loop(1, 2, sum_step, 0)
    give_dx()
    lax.fori_loop(2, half, sum_step, 0)
    partial(dp, 0)

    rows_arrived(2, ro_in)

    def combine(c, total):
        at = pl.ds(pl.multiple_of(c * block, block), block)
        rows_here = ro_in[:, at]
        moe_out[:, at] = (
            dot(high_t[...], rows_here, ((1,), (0,))) + dot(low_t[...], rows_here, ((1,), (0,)))
        ).astype(BF16)
        return total + dot(rows_here, out_grad[:, at], ((1,), (1,)))

    products = lax.fori_loop(0, width // block, combine, jnp.zeros((slots, tok), F32))
    for r in range(3):
        gate_grads[r : r + 1, :] = jnp.sum(
            jnp.where(slot_row == target[r], products, 0.0), axis=0, keepdims=True
        )
    rows_arrived(3, dx_in)

    def combine_dx(c, carry):
        at = pl.ds(pl.multiple_of(c * block, block), block)
        tokens_grad[:, at] = dot(place_t[...], dx_in[:, at], ((1,), (0,))).astype(BF16)
        return carry

    lax.fori_loop(0, width // block, combine_dx, 0)

    arrived(1)
    for ch in range(CHUNKS):
        for way in (0, 1):
            sum_arrived(way, half - 1, ch)
    w_base = dp * rows

    def adam(c, carry):
        at = pl.ds(pl.multiple_of(c * SLOT, SLOT), SLOT)
        grad = (
            part[0, at]
            + sum_in[0, half - 1, at].astype(F32)
            + sum_in[1, half - 1, at].astype(F32)
        )
        first = beta_one * moments[0, at].astype(F32) + (1.0 - beta_one) * grad
        second = beta_two * moments[1, at].astype(F32) + (1.0 - beta_two) * grad * grad
        old = weights[pl.ds(pl.multiple_of(w_base + c * SLOT, SLOT), SLOT), :].astype(F32)
        w_new[at, :] = (old - learn_rate * first / (jnp.sqrt(second) + adam_eps)).astype(BF16)
        m_new[at, :] = first.astype(BF16)
        v_new[at, :] = second.astype(BF16)
        return carry

    lax.fori_loop(0, rows // SLOT, adam, 0)

    for n, ref in enumerate((x_send, g_send, ro_send, dx_send)):
        await_bytes(ref.at[pl.ds(0, others * SLOT)], a2a_s.at[n])
    for a in range(2):
        hops_sent(a)
    for ch in range(CHUNKS):
        at = pl.ds(ch * part_rows, part_rows)
        for way in (0, 1):

            def left_here(k, carry):
                await_bytes(sum_send.at[way, k, at], ag_s.at[way, k, ch])
                await_bytes(sum_send.at[way, k + 1, at], rs_s.at[way, k + 1, ch])
                return carry

            lax.fori_loop(0, half - 1, left_here, 0)
        way = 0 if on_far(0, ch) else 1
        await_bytes(sum_send.at[way, half - 1, at], ag_s.at[way, half - 1, ch])
        await_bytes(sum_send.at[way, 0, at], rs_s.at[way, 0, ch])


def shards(
    grid,
    tokens,
    route_gates,
    expert_ids,
    owner_now,
    owner_next,
    out_grad,
    expert_weights,
    first_moment,
    second_moment,
):
    groups, experts = lax.axis_size("dp"), lax.axis_size("expert")
    tok, width = tokens.shape
    _, rows, cols = expert_weights.shape
    hid = cols // 3
    slots = experts * SLOT
    half = groups // 2
    matches = owner_next[None, :] == jnp.arange(experts, dtype=jnp.int32)[:, None]
    source = jnp.sum(jnp.where(matches, owner_now[None, :], 0), axis=1)
    vmem = pl.BlockSpec(memory_space=pltpu.VMEM)
    dma = pltpu.SemaphoreType.DMA
    state = jax.ShapeDtypeStruct((rows, cols), BF16)
    result = pl.pallas_call(
        functools.partial(kernel, (groups, experts, *grid)),
        out_shape=(
            jax.ShapeDtypeStruct((tok, width), BF16),
            jax.ShapeDtypeStruct((tok, width), BF16),
            jax.ShapeDtypeStruct(route_gates.shape[::-1], F32),
            state,
            state,
            state,
        ),
        in_specs=[pl.BlockSpec(memory_space=pltpu.SMEM)]
        + [vmem] * 6
        + [pl.BlockSpec(memory_space=pl.ANY)] * 2,
        out_specs=(vmem,) * 6,
        scratch_shapes=[
            pltpu.VMEM((slots, width), BF16),
            pltpu.VMEM((slots, width), BF16),
            pltpu.VMEM((slots, width), BF16),
            pltpu.VMEM((slots, width), BF16),
            pltpu.VMEM((width, cols), BF16),
            pltpu.VMEM((slots, cols), F32),
            pltpu.VMEM((slots, hid), BF16),
            pltpu.VMEM((slots, 2 * hid), BF16),
            pltpu.VMEM((slots, width), BF16),
            pltpu.VMEM((slots, width), BF16),
            pltpu.VMEM((slots, width), BF16),
            pltpu.VMEM((slots, width), BF16),
            pltpu.VMEM((2, half, rows, cols), BF16),
            pltpu.VMEM((2, half, rows, cols), BF16),
            pltpu.VMEM((2, rows, cols), F32),
            pltpu.VMEM((slots, tok), BF16),
            pltpu.VMEM((tok, slots), BF16),
            pltpu.VMEM((tok, slots), BF16),
            pltpu.VMEM((tok, slots), BF16),
            pltpu.VMEM((slots, 1), F32),
            pltpu.VMEM((experts, SLOT, WIDE), BF16),
            pltpu.VMEM((experts, SLOT, NARROW), BF16),
            pltpu.VMEM((experts, SLOT, WIDE), BF16),
            pltpu.VMEM((experts, SLOT, NARROW), BF16),
            pltpu.VMEM((experts, 2, SLOT, WIDE), BF16),
            pltpu.VMEM((experts, 2, SLOT, NARROW), BF16),
            pltpu.VMEM((experts, 2, SLOT, WIDE), BF16),
            pltpu.VMEM((experts, 2, SLOT, NARROW), BF16),
            pltpu.VMEM((2, rows, cols), BF16),
            pltpu.VMEM((2, rows, cols), BF16),
            dma((2,)),
            dma((4,)),
            dma((4,)),
            dma((2, 2)),
            dma((2, 2)),
            dma((2, 2)),
            dma((2, 2)),
            dma((2, half, CHUNKS)),
            dma((2, half, CHUNKS)),
            dma((2, half, CHUNKS)),
            dma((2, half, CHUNKS)),
        ],
        compiler_params=pltpu.CompilerParams(
            collective_id=0, has_side_effects=True, vmem_limit_bytes=60 * 2**20
        ),
        name="moe_step",
    )(
        source,
        tokens,
        route_gates.T,
        expert_ids.T,
        owner_next[None, :],
        out_grad,
        expert_weights[0],
        first_moment[0],
        second_moment[0],
    )
    moe_out, tokens_grad, gate_grads, w_new, m_new, v_new = result
    return (moe_out, tokens_grad, gate_grads.T, w_new[None], m_new[None], v_new[None])


def solution(mesh):
    pairs = mesh.shape["expert"] // 2
    ys = 1
    while ys * ys * 4 <= pairs:
        ys *= 2
    by_token = P(("dp", "expert"), None)
    by_state = P("expert", "dp", None)
    return jax.shard_map(
        functools.partial(shards, (pairs // ys, ys)),
        mesh=mesh,
        in_specs=(by_token,) * 3 + (P(), P()) + (by_token,) + (by_state,) * 3,
        out_specs=(by_token,) * 3 + (by_state,) * 3,
        check_vma=False,
    )
```

```python
import functools

import jax
import jax.numpy as jnp
from jax import lax
from jax.experimental import pallas as pl
from jax.experimental.pallas import tpu as pltpu
from jax.sharding import PartitionSpec as P

MESH = pl.DeviceIdType.MESH
BF16 = jnp.bfloat16
F32 = jnp.float32

beta_one = 0.9
beta_two = 0.95
learn_rate = 0.003
adam_eps = 1e-08

SLOT = 16
WIDE, NARROW = 256, 128
X_STEPS, G_STEPS = 2, 4
CHUNKS = 2


def dot(a, b, dims):
    return lax.dot_general(a, b, (dims, ((), ())), preferred_element_type=F32)


def kernel(
    cfg,
    source,
    tokens,
    gates,
    ids,
    owner_next,
    out_grad,
    w_old,
    m_old,
    v_old,
    moe_out,
    tokens_grad,
    gate_grads,
    w_new,
    m_new,
    v_new,
    x_send,
    g_send,
    x_in,
    g_in,
    weights,
    gate_up,
    act,
    pre,
    ro_send,
    dx_send,
    ro_in,
    dx_in,
    sum_send,
    sum_in,
    part,
    place,
    place_t,
    high_t,
    low_t,
    gate_of,
    hop_w_a,
    hop_w_b,
    out_w_a,
    out_w_b,
    hop_m,
    hop_v,
    out_m,
    out_v,
    moments_old,
    moments,
    load_s,
    a2a_s,
    a2a_r,
    hop1_s,
    hop1_r,
    hop2_s,
    hop2_r,
    ag_s,
    ag_r,
    rs_s,
    rs_r,
):
    groups, experts, xs, ys = cfg
    hop_a, hop_b, out_a, out_b = (hop_w_a,), (hop_w_b,), (out_w_a,), (out_w_b,)
    hops, outs = (None, hop_m, hop_v), (None, out_m, out_v)
    dp = lax.axis_index("dp")
    me = lax.axis_index("expert")
    tok, width = tokens.shape
    rows, cols = w_old.shape
    hid = cols // 3
    slots = experts * SLOT
    others = experts - 1
    n_wide = cols // WIDE
    n_row = rows // SLOT
    half = groups // 2
    part_rows = rows // CHUNKS
    right = lax.rem(dp + 1, groups)
    left = lax.rem(dp + groups - 1, groups)
    y_bits = ys.bit_length()
    low_bits = (1 << y_bits) - 1

    def peer(i):
        off = (i * 11) & (experts - 1)
        x_part = ((me >> y_bits) + (off >> y_bits)) & (xs - 1)
        y_part = ((me & low_bits & ~1) + (off & low_bits & ~1)) & low_bits
        return (x_part << y_bits) | y_part | ((me ^ off) & 1)

    def each_peer(low, high, body):
        def step(i, carry):
            body(peer(i))
            return carry

        lax.fori_loop(low, high, step, 0)

    def remote(src, dst, ssem, rsem, device):
        pltpu.make_async_remote_copy(
            src_ref=src,
            dst_ref=dst,
            send_sem=ssem,
            recv_sem=rsem,
            device_id=device,
            device_id_type=MESH,
        ).start()

    def await_bytes(ref, sem):
        pltpu.make_async_copy(ref, ref, sem).wait()

    loads = [
        pltpu.make_async_copy(ref, moments_old.at[n], load_s.at[n])
        for n, ref in enumerate((m_old, v_old))
    ]
    for load in loads:
        load.start()

    barrier = pltpu.get_barrier_semaphore()
    each_peer(
        1,
        experts,
        lambda d: pl.semaphore_signal(
            barrier, inc=1, device_id=(dp, d), device_id_type=MESH
        ),
    )
    for z in (left, right):
        pl.semaphore_signal(barrier, inc=1, device_id=(z, me), device_id_type=MESH)
    pl.semaphore_wait(barrier, experts + 1)

    shift = n_wide.bit_length() - 1

    def piece(ref, lead, relay, base=0):
        return ref.at[
            (
                *lead,
                pl.ds(pl.multiple_of(base + (relay >> shift) * SLOT, SLOT), SLOT),
                pl.ds(pl.multiple_of((relay & (n_wide - 1)) * WIDE, WIDE), WIDE),
            )
        ]

    def rest(ref, lead, relay, base=0):
        return ref.at[
            (
                *lead,
                pl.ds(pl.multiple_of(base + (relay >> shift) * SLOT, SLOT), SLOT),
                pl.ds(n_wide * WIDE, NARROW),
            )
        ]

    def narrow(a, device):
        return (device & (n_wide - 1)) == a % n_wide

    leads = ((),)

    def hop_one(a, ref):
        def one(d):
            remote(
                piece(ref, leads[a], d), hop_a[a].at[me], hop1_s.at[a, 0], hop1_r.at[a, 0], (dp, d)
            )

            @pl.when(narrow(a, d))
            def _():
                remote(
                    rest(ref, leads[a], d), hop_b[a].at[me], hop1_s.at[a, 1], hop1_r.at[a, 1], (dp, d)
                )

        each_peer(1, experts, one)
        hop_a[a][me] = piece(ref, leads[a], me)[...]

        @pl.when(narrow(a, me))
        def _():
            hop_b[a][me] = rest(ref, leads[a], me)[...]

    def hop_two(a, ref, base):
        def pass_on(n, hop, out, part_of):
            await_bytes(hop.at[pl.ds(0, others)], hop1_r.at[a, n])

            def pick(s, carry):
                out[s] = hop[source[s]]
                return carry

            lax.fori_loop(0, experts, pick, 0)
            each_peer(
                1,
                experts,
                lambda d: remote(
                    out.at[d],
                    part_of(ref, leads[a], me, base),
                    hop2_s.at[a, n],
                    hop2_r.at[a, n],
                    (dp, d),
                ),
            )
            part_of(ref, leads[a], me, base)[...] = out[me]

        pass_on(0, hop_a[a], out_a[a], piece)

        @pl.when(narrow(a, me))
        def _():
            pass_on(1, hop_b[a], out_b[a], rest)

    def narrow_wait(a, sem):
        @pl.when(narrow(a, me))
        def _():
            await_bytes(hop_b[a].at[pl.ds(0, n_row - 1)], sem)

        @pl.when(jnp.logical_not(narrow(a, me)))
        def _():
            await_bytes(hop_b[a].at[pl.ds(0, n_row)], sem)

    def arrived(a):
        await_bytes(hop_a[a].at[pl.ds(0, others)], hop2_r.at[a, 0])
        narrow_wait(a, hop2_r.at[a, 1])

    def hops_sent(a):
        await_bytes(hop_a[a].at[pl.ds(0, others)], hop1_s.at[a, 0])
        narrow_wait(a, hop1_s.at[a, 1])
        await_bytes(hop_a[a].at[pl.ds(0, others)], hop2_s.at[a, 0])

        @pl.when(narrow(a, me))
        def _():
            await_bytes(hop_b[a].at[pl.ds(0, others)], hop2_s.at[a, 1])

    def relay(a, p):
        if n_row * 4 != experts:
            return p
        x = p // 2
        return (x * ys + 2 * (p % 2) + (x + a) % 2) * 2 + a // 2

    relays = [[relay(a, p) for p in range(n_row)] for a in range(3)]
    my_piece = [sum(jnp.where(me == d, p, 0) for p, d in enumerate(ds)) for ds in relays]
    is_relay = [sum(jnp.where(me == d, 1, 0) for d in ds) > 0 for ds in relays]

    def rows_at(ref, p, base=0):
        return ref.at[pl.ds(pl.multiple_of(base + p * SLOT, SLOT), SLOT)]

    def moment_hop_one(a, ref):
        for p, d in enumerate(relays[a]):

            @pl.when(me != d)
            def _():
                remote(rows_at(ref, p), hops[a].at[me], hop1_s.at[a, 0], hop1_r.at[a, 0], (dp, d))

            @pl.when(me == d)
            def _():
                hops[a][me] = rows_at(ref, p)[...]

    def moment_hop_two(a, ref, base):
        hop, out = hops[a], outs[a]

        @pl.when(is_relay[a])
        def _():
            await_bytes(hop.at[pl.ds(0, others)], hop1_r.at[a, 0])

            def pick(s, carry):
                out[s] = hop[source[s]]
                return carry

            lax.fori_loop(0, experts, pick, 0)
            goal = rows_at(ref, my_piece[a], base)
            each_peer(
                1,
                experts,
                lambda d: remote(out.at[d], goal, hop2_s.at[a, 0], hop2_r.at[a, 0], (dp, d)),
            )
            goal[...] = out[me]

    def pieces_wait(a, sem):
        @pl.when(is_relay[a])
        def _():
            await_bytes(hops[a].at[pl.ds(0, n_row - 1)], sem)

        @pl.when(jnp.logical_not(is_relay[a]))
        def _():
            await_bytes(hops[a].at[pl.ds(0, n_row)], sem)

    def moment_arrived(a):
        pieces_wait(a, hop2_r.at[a, 0])

    def moment_hops_sent(a):
        pieces_wait(a, hop1_s.at[a, 0])

        @pl.when(is_relay[a])
        def _():
            await_bytes(outs[a].at[pl.ds(0, others)], hop2_s.at[a, 0])

    def zone(z, ch=0, size=None):
        start = ((z + groups) & (groups - 1)) * rows + ch * part_rows
        return pl.ds(pl.multiple_of(start, part_rows), size or rows)

    def on_far(way, ch):
        return (ch < CHUNKS // 2) == (way == 0)

    hop_one(0, w_old)

    expert_row = lax.broadcasted_iota(jnp.int32, (experts, tok), 0)
    hits = [(ids[r : r + 1, :] == expert_row).astype(F32) for r in range(3)]
    before = lax.broadcasted_iota(jnp.int32, (tok, tok), 0) < lax.broadcasted_iota(
        jnp.int32, (tok, tok), 1
    )
    position = dot(
        (hits[0] + hits[1] + hits[2]).astype(BF16),
        before.astype(F32).astype(BF16),
        ((1,), (0,)),
    )
    diagonal = lax.broadcasted_iota(jnp.int32, (experts, experts), 0) == lax.broadcasted_iota(
        jnp.int32, (experts, experts), 1
    )
    holder = jnp.sum(
        jnp.where(diagonal, owner_next[...].astype(F32), 0.0), axis=1, keepdims=True
    )
    row_at = holder * SLOT + position
    target = [
        jnp.sum(h * row_at, axis=0, keepdims=True).astype(jnp.int32) for h in hits
    ]
    slot_row = lax.broadcasted_iota(jnp.int32, (slots, tok), 0)
    spread = jnp.zeros((slots, tok), F32)
    weighted = jnp.zeros((slots, tok), F32)
    for r in range(3):
        here = slot_row == target[r]
        spread = spread + here.astype(F32)
        weighted = weighted + jnp.where(here, gates[r : r + 1, :], 0.0)
    place[...] = spread.astype(BF16)
    block = min(256, width)

    def gather_x(c, carry):
        at = pl.ds(pl.multiple_of(c * block, block), block)
        x_send[:, at] = dot(place[...], tokens[:, at], ((1,), (0,))).astype(BF16)
        return carry

    lax.fori_loop(0, width // block, gather_x, 0)

    hop_two(0, weights, dp * rows)

    mine = pl.ds(pl.multiple_of(me * SLOT, SLOT), SLOT)

    def send_rows(n, src, dst, low, high):
        each_peer(
            low,
            high,
            lambda d: remote(
                src.at[pl.ds(pl.multiple_of(d * SLOT, SLOT), SLOT)],
                dst.at[mine],
                a2a_s.at[n],
                a2a_r.at[n],
                (dp, d),
            ),
        )

    def rows_arrived(n, ref):
        await_bytes(ref.at[pl.ds(0, others * SLOT)], a2a_r.at[n])

    def share(steps, k):
        per = -(-others // steps)
        return 1 + jnp.minimum(k * per, others), 1 + jnp.minimum((k + 1) * per, others)

    send_rows(0, x_send, x_in, *share(X_STEPS, 0))
    x_in[mine, :] = x_send[mine, :]

    gate_of[...] = jnp.sum(weighted, axis=1, keepdims=True)

    def gather_g(c, carry):
        at = pl.ds(pl.multiple_of(c * block, block), block)
        g_send[:, at] = (
            dot(place[...], out_grad[:, at], ((1,), (0,))) * gate_of[...]
        ).astype(BF16)
        return carry

    lax.fori_loop(0, width // block, gather_g, 0)
    g_in[mine, :] = g_send[mine, :]

    def gather_copy(way, k, ch):
        at = zone(dp - k if way == 0 else dp + k, ch, part_rows)
        remote(
            weights.at[at],
            weights.at[at],
            ag_s.at[way, k, ch],
            ag_r.at[way, k, ch],
            (right if way == 0 else left, me),
        )

    def gathered(way, k, ch):
        z = dp - k - 1 if way == 0 else dp + k + 1
        await_bytes(weights.at[zone(z, ch, part_rows)], ag_r.at[way, k, ch])

    arrived(0)
    for ch in range(CHUNKS):
        for way in (0, 1):
            gather_copy(way, 0, ch)

    for k in range(1, X_STEPS):
        send_rows(0, x_send, x_in, *share(X_STEPS, k))

    def gather_step(k, carry):
        for ch in range(CHUNKS):
            for way in (0, 1):
                gathered(way, k, ch)

                if on_far(way, ch):
                    gather_copy(way, k + 1, ch)
                else:

                    @pl.when(k + 1 < half - 1)
                    def _():
                        gather_copy(way, k + 1, ch)

        @pl.when(k < G_STEPS)
        def _():
            send_rows(1, g_send, g_in, *share(G_STEPS, k))

        return carry

    lax.fori_loop(0, half - 1, gather_step, 0)
    for k in range(half - 1, G_STEPS):
        send_rows(1, g_send, g_in, *share(G_STEPS, k))

    for load in loads:
        load.wait()
    moment_hop_one(1, moments_old.at[0])
    moment_hop_one(2, moments_old.at[1])

    weighted_t = weighted.T
    high = weighted_t.astype(BF16)
    high_t[...] = high
    low_t[...] = (weighted_t - high.astype(F32)).astype(BF16)
    place_t[...] = spread.T.astype(BF16)

    def hidden_sums(rows_here, base, zs, first):
        step = min(256, hid) if base == 0 else hid
        for c in range(base, 2 * hid if base == 0 else 3 * hid, step):
            total = None
            for z in zs:
                term = dot(
                    jnp.concatenate([rows_here[:, zone(i)] for i in z], axis=1),
                    jnp.concatenate([weights[zone(i), c : c + step] for i in z], axis=0),
                    ((1,), (0,)),
                )
                total = term if total is None else total + term
            gate_up[:, c : c + step] = total if first else gate_up[:, c : c + step] + total

    near = [dp + half + 1 + n for n in range(groups - 1)]
    near = [near[n : n + 2] for n in range(0, groups - 1, 2)]
    rows_arrived(0, x_in)
    hidden_sums(x_in, 0, near, True)
    rows_arrived(1, g_in)
    hidden_sums(g_in, 2 * hid, near, True)
    moment_hop_two(1, moments.at[0], 0)
    moment_hop_two(2, moments.at[1], 0)
    for ch in range(CHUNKS):
        gathered(0 if on_far(0, ch) else 1, half - 1, ch)
    hidden_sums(x_in, 0, [[dp + half]], False)

    height = min(64, slots)

    def each_part(body):
        def step(c, carry):
            body(pl.ds(pl.multiple_of(c * height, height), height))
            return carry

        lax.fori_loop(0, slots // height, step, 0)

    def forward(at):
        gate = gate_up[at, 0:hid]
        act[at, :] = (gate * jax.nn.sigmoid(gate) * gate_up[at, hid : 2 * hid]).astype(BF16)

    each_part(forward)

    def route_out(c, carry):
        at = pl.ds(pl.multiple_of(c * block, block), block)
        ro_send[:, at] = dot(act[...], weights[at, 2 * hid : 3 * hid], ((1,), (1,))).astype(BF16)
        return carry

    lax.fori_loop(0, width // block, route_out, 0)
    send_rows(2, ro_send, ro_in, 1, experts)
    ro_in[mine, :] = ro_send[mine, :]

    hidden_sums(g_in, 2 * hid, [[dp + half]], False)

    def backward(at):
        gate = gate_up[at, 0:hid]
        up = gate_up[at, hid : 2 * hid]
        grad = gate_up[at, 2 * hid : 3 * hid]
        sig = jax.nn.sigmoid(gate)
        pre[at, 0:hid] = (grad * up * sig * (1.0 + gate * (1.0 - sig))).astype(BF16)
        pre[at, hid : 2 * hid] = (grad * (gate * sig)).astype(BF16)

    each_part(backward)

    def partial(*zs):
        x_side = jnp.concatenate([x_in[:, zone(z)] for z in zs], axis=1)
        g_side = jnp.concatenate([g_in[:, zone(z)] for z in zs], axis=1)
        high = len(zs) * rows
        part[0:high, 0 : 2 * hid] = dot(x_side, pre[...], ((0,), (0,)))
        part[0:high, 2 * hid : 3 * hid] = dot(g_side, act[...], ((0,), (0,)))

    def sum_copy(way, k, ch):
        at = pl.ds(ch * part_rows, part_rows)
        remote(
            sum_send.at[way, k, at],
            sum_in.at[way, k, at],
            rs_s.at[way, k, ch],
            rs_r.at[way, k, ch],
            (right if way == 0 else left, me),
        )

    def sum_arrived(way, k, ch):
        at = pl.ds(ch * part_rows, part_rows)
        await_bytes(sum_in.at[way, k, at], rs_r.at[way, k, ch])

    partial(dp + half)
    for ch in range(CHUNKS):
        way = 0 if on_far(0, ch) else 1
        at = pl.ds(ch * part_rows, part_rows)
        sum_send[way, 0, at] = part[at, :].astype(BF16)
        sum_copy(way, 0, ch)

    def sum_step(k, carry):
        partial(dp + half - k, dp - half + k)

        for ch in range(CHUNKS):
            at = pl.ds(ch * part_rows, part_rows)
            for way in (0, 1):
                own = pl.ds(way * rows + ch * part_rows, part_rows)

                def add():
                    sum_arrived(way, k - 1, ch)
                    sum_send[way, k, at] = (
                        part[own, :] + sum_in[way, k - 1, at].astype(F32)
                    ).astype(BF16)

                if on_far(way, ch):
                    add()
                else:
                    pl.when(k > 1)(add)

                    @pl.when(k == 1)
                    def _():
                        sum_send[way, k, at] = part[own, :].astype(BF16)

                sum_copy(way, k, ch)
        return carry

    def give_dx():
        def dx_out(c, carry):
            at = pl.ds(pl.multiple_of(c * block, block), block)
            dx_send[:, at] = dot(pre[...], weights[at, 0 : 2 * hid], ((1,), (1,))).astype(BF16)
            return carry

        lax.fori_loop(0, width // block, dx_out, 0)
        send_rows(3, dx_send, dx_in, 1, experts)
        dx_in[mine, :] = dx_send[mine, :]

    lax.fori_loop(1, 2, sum_step, 0)
    give_dx()
    lax.fori_loop(2, half, sum_step, 0)
    partial(dp)

    rows_arrived(2, ro_in)

    def combine(c, total):
        at = pl.ds(pl.multiple_of(c * block, block), block)
        rows_here = ro_in[:, at]
        moe_out[:, at] = (
            dot(high_t[...], rows_here, ((1,), (0,))) + dot(low_t[...], rows_here, ((1,), (0,)))
        ).astype(BF16)
        return total + dot(rows_here, out_grad[:, at], ((1,), (1,)))

    products = lax.fori_loop(0, width // block, combine, jnp.zeros((slots, tok), F32))
    for r in range(3):
        gate_grads[r : r + 1, :] = jnp.sum(
            jnp.where(slot_row == target[r], products, 0.0), axis=0, keepdims=True
        )
    moment_arrived(1)
    moment_arrived(2)
    for ch in range(CHUNKS):
        for way in (0, 1):
            sum_arrived(way, half - 1, ch)
    w_base = dp * rows

    def adam(c, carry):
        at = pl.ds(pl.multiple_of(c * SLOT, SLOT), SLOT)
        grad = (
            part[at, :]
            + sum_in[0, half - 1, at].astype(F32)
            + sum_in[1, half - 1, at].astype(F32)
        )
        first = beta_one * moments[0, at].astype(F32) + (1.0 - beta_one) * grad
        second = beta_two * moments[1, at].astype(F32) + (1.0 - beta_two) * grad * grad
        old = weights[pl.ds(pl.multiple_of(w_base + c * SLOT, SLOT), SLOT), :].astype(F32)
        w_new[at, :] = (old - learn_rate * first / (jnp.sqrt(second) + adam_eps)).astype(BF16)
        m_new[at, :] = first.astype(BF16)
        v_new[at, :] = second.astype(BF16)
        return carry

    lax.fori_loop(0, rows // SLOT, adam, 0)

    rows_arrived(3, dx_in)

    def combine_dx(c, carry):
        at = pl.ds(pl.multiple_of(c * block, block), block)
        tokens_grad[:, at] = dot(place_t[...], dx_in[:, at], ((1,), (0,))).astype(BF16)
        return carry

    lax.fori_loop(0, width // block, combine_dx, 0)

    for n, ref in enumerate((x_send, g_send, ro_send, dx_send)):
        await_bytes(ref.at[pl.ds(0, others * SLOT)], a2a_s.at[n])
    hops_sent(0)
    for a in (1, 2):
        moment_hops_sent(a)
    for ch in range(CHUNKS):
        at = pl.ds(ch * part_rows, part_rows)
        for way in (0, 1):

            def left_here(k, carry):
                await_bytes(sum_send.at[way, k, at], ag_s.at[way, k, ch])
                await_bytes(sum_send.at[way, k + 1, at], rs_s.at[way, k + 1, ch])
                return carry

            lax.fori_loop(0, half - 1, left_here, 0)
        way = 0 if on_far(0, ch) else 1
        await_bytes(sum_send.at[way, half - 1, at], ag_s.at[way, half - 1, ch])
        await_bytes(sum_send.at[way, 0, at], rs_s.at[way, 0, ch])


def shards(
    grid,
    tokens,
    route_gates,
    expert_ids,
    owner_now,
    owner_next,
    out_grad,
    expert_weights,
    first_moment,
    second_moment,
):
    groups, experts = lax.axis_size("dp"), lax.axis_size("expert")
    tok, width = tokens.shape
    _, rows, cols = expert_weights.shape
    hid = cols // 3
    slots = experts * SLOT
    half = groups // 2
    matches = owner_next[None, :] == jnp.arange(experts, dtype=jnp.int32)[:, None]
    source = jnp.sum(jnp.where(matches, owner_now[None, :], 0), axis=1)
    vmem = pl.BlockSpec(memory_space=pltpu.VMEM)
    dma = pltpu.SemaphoreType.DMA
    state = jax.ShapeDtypeStruct((rows, cols), BF16)
    result = pl.pallas_call(
        functools.partial(kernel, (groups, experts, *grid)),
        out_shape=(
            jax.ShapeDtypeStruct((tok, width), BF16),
            jax.ShapeDtypeStruct((tok, width), BF16),
            jax.ShapeDtypeStruct(route_gates.shape[::-1], F32),
            state,
            state,
            state,
        ),
        in_specs=[pl.BlockSpec(memory_space=pltpu.SMEM)]
        + [vmem] * 6
        + [pl.BlockSpec(memory_space=pl.ANY)] * 2,
        out_specs=(vmem,) * 6,
        scratch_shapes=[
            pltpu.VMEM((slots, width), BF16),
            pltpu.VMEM((slots, width), BF16),
            pltpu.VMEM((slots, width), BF16),
            pltpu.VMEM((slots, width), BF16),
            pltpu.VMEM((width, cols), BF16),
            pltpu.VMEM((slots, cols), F32),
            pltpu.VMEM((slots, hid), BF16),
            pltpu.VMEM((slots, 2 * hid), BF16),
            pltpu.VMEM((slots, width), BF16),
            pltpu.VMEM((slots, width), BF16),
            pltpu.VMEM((slots, width), BF16),
            pltpu.VMEM((slots, width), BF16),
            pltpu.VMEM((2, half, rows, cols), BF16),
            pltpu.VMEM((2, half, rows, cols), BF16),
            pltpu.VMEM((2 * rows, cols), F32),
            pltpu.VMEM((slots, tok), BF16),
            pltpu.VMEM((tok, slots), BF16),
            pltpu.VMEM((tok, slots), BF16),
            pltpu.VMEM((tok, slots), BF16),
            pltpu.VMEM((slots, 1), F32),
            pltpu.VMEM((experts, SLOT, WIDE), BF16),
            pltpu.VMEM((experts, SLOT, NARROW), BF16),
            pltpu.VMEM((experts, SLOT, WIDE), BF16),
            pltpu.VMEM((experts, SLOT, NARROW), BF16),
            *[pltpu.VMEM((experts, SLOT, cols), BF16)] * 4,
            pltpu.VMEM((2, rows, cols), BF16),
            pltpu.VMEM((2, rows, cols), BF16),
            dma((2,)),
            dma((4,)),
            dma((4,)),
            dma((3, 2)),
            dma((3, 2)),
            dma((3, 2)),
            dma((3, 2)),
            dma((2, half, CHUNKS)),
            dma((2, half, CHUNKS)),
            dma((2, half, CHUNKS)),
            dma((2, half, CHUNKS)),
        ],
        compiler_params=pltpu.CompilerParams(
            collective_id=0, has_side_effects=True, vmem_limit_bytes=60 * 2**20
        ),
        name="moe_step",
    )(
        source,
        tokens,
        route_gates.T,
        expert_ids.T,
        owner_next[None, :],
        out_grad,
        expert_weights[0],
        first_moment[0],
        second_moment[0],
    )
    moe_out, tokens_grad, gate_grads, w_new, m_new, v_new = result
    return (moe_out, tokens_grad, gate_grads.T, w_new[None], m_new[None], v_new[None])


def solution(mesh):
    pairs = mesh.shape["expert"] // 2
    ys = 1
    while ys * ys * 4 <= pairs:
        ys *= 2
    by_token = P(("dp", "expert"), None)
    by_state = P("expert", "dp", None)
    return jax.shard_map(
        functools.partial(shards, (pairs // ys, ys)),
        mesh=mesh,
        in_specs=(by_token,) * 3 + (P(), P()) + (by_token,) + (by_state,) * 3,
        out_specs=(by_token,) * 3 + (by_state,) * 3,
        check_vma=False,
    )
```

```python
import functools

import jax
import jax.numpy as jnp
from jax import lax
from jax.experimental import pallas as pl
from jax.experimental.pallas import tpu as pltpu
from jax.sharding import PartitionSpec as P

MESH = pl.DeviceIdType.MESH
BF16 = jnp.bfloat16
F32 = jnp.float32

beta_one = 0.9
beta_two = 0.95
learn_rate = 0.003
adam_eps = 1e-08

SLOT = 16
WIDE, NARROW = 256, 128
X_STEPS, G_STEPS = 2, 4
CHUNKS = 2


def dot(a, b, dims):
    return lax.dot_general(a, b, (dims, ((), ())), preferred_element_type=F32)


def kernel(
    cfg,
    source,
    tokens,
    gates,
    ids,
    owner_next,
    out_grad,
    w_old,
    m_old,
    v_old,
    moe_out,
    tokens_grad,
    gate_grads,
    grad_sum,
    w_moved,
    m_moved,
    v_moved,
    x_send,
    g_send,
    x_in,
    g_in,
    weights,
    gate_up,
    act,
    pre,
    ro_send,
    dx_send,
    ro_in,
    dx_in,
    sum_send,
    sum_in,
    part,
    place,
    place_t,
    high_t,
    low_t,
    gate_of,
    hop_w_a,
    hop_w_b,
    out_w_a,
    out_w_b,
    hop_m,
    hop_v,
    out_m,
    out_v,
    moments_old,
    moments,
    load_s,
    a2a_s,
    a2a_r,
    hop1_s,
    hop1_r,
    hop2_s,
    hop2_r,
    ag_s,
    ag_r,
    rs_s,
    rs_r,
):
    groups, experts, xs, ys = cfg
    hop_a, hop_b, out_a, out_b = (hop_w_a,), (hop_w_b,), (out_w_a,), (out_w_b,)
    hops, outs = (None, hop_m, hop_v), (None, out_m, out_v)
    dp = lax.axis_index("dp")
    me = lax.axis_index("expert")
    tok, width = tokens.shape
    rows, cols = w_old.shape
    hid = cols // 3
    slots = experts * SLOT
    others = experts - 1
    n_wide = cols // WIDE
    n_row = rows // SLOT
    half = groups // 2
    part_rows = rows // CHUNKS
    right = lax.rem(dp + 1, groups)
    left = lax.rem(dp + groups - 1, groups)
    y_bits = ys.bit_length()
    low_bits = (1 << y_bits) - 1

    def peer(i):
        off = (i * 5) & (experts - 1)
        x_part = ((me >> y_bits) + (off >> y_bits)) & (xs - 1)
        y_part = ((me & low_bits & ~1) + (off & low_bits & ~1)) & low_bits
        return (x_part << y_bits) | y_part | ((me ^ off) & 1)

    def each_peer(low, high, body):
        def step(i, carry):
            body(peer(i))
            return carry

        lax.fori_loop(low, high, step, 0)

    def remote(src, dst, ssem, rsem, device):
        pltpu.make_async_remote_copy(
            src_ref=src,
            dst_ref=dst,
            send_sem=ssem,
            recv_sem=rsem,
            device_id=device,
            device_id_type=MESH,
        ).start()

    def await_bytes(ref, sem):
        pltpu.make_async_copy(ref, ref, sem).wait()

    loads = [
        pltpu.make_async_copy(ref, moments_old.at[n], load_s.at[n])
        for n, ref in enumerate((m_old, v_old))
    ]
    for load in loads:
        load.start()

    barrier = pltpu.get_barrier_semaphore()
    each_peer(
        1,
        experts,
        lambda d: pl.semaphore_signal(
            barrier, inc=1, device_id=(dp, d), device_id_type=MESH
        ),
    )
    for z in (left, right):
        pl.semaphore_signal(barrier, inc=1, device_id=(z, me), device_id_type=MESH)
    pl.semaphore_wait(barrier, experts + 1)

    shift = n_wide.bit_length() - 1

    def piece(ref, lead, relay, base=0):
        return ref.at[
            (
                *lead,
                pl.ds(pl.multiple_of(base + (relay >> shift) * SLOT, SLOT), SLOT),
                pl.ds(pl.multiple_of((relay & (n_wide - 1)) * WIDE, WIDE), WIDE),
            )
        ]

    def rest(ref, lead, relay, base=0):
        return ref.at[
            (
                *lead,
                pl.ds(pl.multiple_of(base + (relay >> shift) * SLOT, SLOT), SLOT),
                pl.ds(n_wide * WIDE, NARROW),
            )
        ]

    def narrow(a, device):
        return (device & (n_wide - 1)) == a % n_wide

    leads = ((),)

    def hop_one(a, ref):
        def one(d):
            remote(
                piece(ref, leads[a], d), hop_a[a].at[me], hop1_s.at[a, 0], hop1_r.at[a, 0], (dp, d)
            )

            @pl.when(narrow(a, d))
            def _():
                remote(
                    rest(ref, leads[a], d), hop_b[a].at[me], hop1_s.at[a, 1], hop1_r.at[a, 1], (dp, d)
                )

        each_peer(1, experts, one)
        hop_a[a][me] = piece(ref, leads[a], me)[...]

        @pl.when(narrow(a, me))
        def _():
            hop_b[a][me] = rest(ref, leads[a], me)[...]

    def hop_two(a, ref, base):
        def pass_on(n, hop, out, part_of):
            await_bytes(hop.at[pl.ds(0, others)], hop1_r.at[a, n])

            def pick(s, carry):
                out[s] = hop[source[s]]
                return carry

            lax.fori_loop(0, experts, pick, 0)
            each_peer(
                1,
                experts,
                lambda d: remote(
                    out.at[d],
                    part_of(ref, leads[a], me, base),
                    hop2_s.at[a, n],
                    hop2_r.at[a, n],
                    (dp, d),
                ),
            )
            part_of(ref, leads[a], me, base)[...] = out[me]

        pass_on(0, hop_a[a], out_a[a], piece)

        @pl.when(narrow(a, me))
        def _():
            pass_on(1, hop_b[a], out_b[a], rest)

    def narrow_wait(a, sem):
        @pl.when(narrow(a, me))
        def _():
            await_bytes(hop_b[a].at[pl.ds(0, n_row - 1)], sem)

        @pl.when(jnp.logical_not(narrow(a, me)))
        def _():
            await_bytes(hop_b[a].at[pl.ds(0, n_row)], sem)

    def arrived(a):
        await_bytes(hop_a[a].at[pl.ds(0, others)], hop2_r.at[a, 0])
        narrow_wait(a, hop2_r.at[a, 1])

    def hops_sent(a):
        await_bytes(hop_a[a].at[pl.ds(0, others)], hop1_s.at[a, 0])
        narrow_wait(a, hop1_s.at[a, 1])
        await_bytes(hop_a[a].at[pl.ds(0, others)], hop2_s.at[a, 0])

        @pl.when(narrow(a, me))
        def _():
            await_bytes(hop_b[a].at[pl.ds(0, others)], hop2_s.at[a, 1])

    def relay(a, p):
        if n_row * 4 != experts:
            return p
        x = p // 2
        return (x * ys + 2 * (p % 2) + (x + a) % 2) * 2 + a // 2

    relays = [[relay(a, p) for p in range(n_row)] for a in range(3)]
    my_piece = [sum(jnp.where(me == d, p, 0) for p, d in enumerate(ds)) for ds in relays]
    is_relay = [sum(jnp.where(me == d, 1, 0) for d in ds) > 0 for ds in relays]

    def rows_at(ref, p, base=0):
        return ref.at[pl.ds(pl.multiple_of(base + p * SLOT, SLOT), SLOT)]

    def moment_hop_one(a, ref):
        for p, d in enumerate(relays[a]):

            @pl.when(me != d)
            def _():
                remote(rows_at(ref, p), hops[a].at[me], hop1_s.at[a, 0], hop1_r.at[a, 0], (dp, d))

            @pl.when(me == d)
            def _():
                hops[a][me] = rows_at(ref, p)[...]

    def moment_hop_two(a, ref, base):
        hop, out = hops[a], outs[a]

        @pl.when(is_relay[a])
        def _():
            await_bytes(hop.at[pl.ds(0, others)], hop1_r.at[a, 0])

            def pick(s, carry):
                out[s] = hop[source[s]]
                return carry

            lax.fori_loop(0, experts, pick, 0)
            goal = rows_at(ref, my_piece[a], base)
            each_peer(
                1,
                experts,
                lambda d: remote(out.at[d], goal, hop2_s.at[a, 0], hop2_r.at[a, 0], (dp, d)),
            )
            goal[...] = out[me]

    def pieces_wait(a, sem):
        @pl.when(is_relay[a])
        def _():
            await_bytes(hops[a].at[pl.ds(0, n_row - 1)], sem)

        @pl.when(jnp.logical_not(is_relay[a]))
        def _():
            await_bytes(hops[a].at[pl.ds(0, n_row)], sem)

    def moment_arrived(a):
        pieces_wait(a, hop2_r.at[a, 0])

    def moment_hops_sent(a):
        pieces_wait(a, hop1_s.at[a, 0])

        @pl.when(is_relay[a])
        def _():
            await_bytes(outs[a].at[pl.ds(0, others)], hop2_s.at[a, 0])

    def zone(z, ch=0, size=None):
        start = ((z + groups) & (groups - 1)) * rows + ch * part_rows
        return pl.ds(pl.multiple_of(start, part_rows), size or rows)

    def on_far(way, ch):
        return (ch < CHUNKS // 2) == (way == 0)

    hop_one(0, w_old)

    expert_row = lax.broadcasted_iota(jnp.int32, (experts, tok), 0)
    hits = [(ids[r : r + 1, :] == expert_row).astype(F32) for r in range(3)]
    before = lax.broadcasted_iota(jnp.int32, (tok, tok), 0) < lax.broadcasted_iota(
        jnp.int32, (tok, tok), 1
    )
    position = dot(
        (hits[0] + hits[1] + hits[2]).astype(BF16),
        before.astype(F32).astype(BF16),
        ((1,), (0,)),
    )
    diagonal = lax.broadcasted_iota(jnp.int32, (experts, experts), 0) == lax.broadcasted_iota(
        jnp.int32, (experts, experts), 1
    )
    holder = jnp.sum(
        jnp.where(diagonal, owner_next[...].astype(F32), 0.0), axis=1, keepdims=True
    )
    row_at = holder * SLOT + position
    target = [
        jnp.sum(h * row_at, axis=0, keepdims=True).astype(jnp.int32) for h in hits
    ]
    slot_row = lax.broadcasted_iota(jnp.int32, (slots, tok), 0)
    spread = jnp.zeros((slots, tok), F32)
    weighted = jnp.zeros((slots, tok), F32)
    for r in range(3):
        here = slot_row == target[r]
        spread = spread + here.astype(F32)
        weighted = weighted + jnp.where(here, gates[r : r + 1, :], 0.0)
    place[...] = spread.astype(BF16)
    block = min(256, width)

    def gather_x(c, carry):
        at = pl.ds(pl.multiple_of(c * block, block), block)
        x_send[:, at] = dot(place[...], tokens[:, at], ((1,), (0,))).astype(BF16)
        return carry

    lax.fori_loop(0, width // block, gather_x, 0)

    hop_two(0, weights, dp * rows)

    mine = pl.ds(pl.multiple_of(me * SLOT, SLOT), SLOT)

    def send_rows(n, src, dst, low, high):
        each_peer(
            low,
            high,
            lambda d: remote(
                src.at[pl.ds(pl.multiple_of(d * SLOT, SLOT), SLOT)],
                dst.at[mine],
                a2a_s.at[n],
                a2a_r.at[n],
                (dp, d),
            ),
        )

    def rows_arrived(n, ref):
        await_bytes(ref.at[pl.ds(0, others * SLOT)], a2a_r.at[n])

    def share(steps, k):
        per = -(-others // steps)
        return 1 + jnp.minimum(k * per, others), 1 + jnp.minimum((k + 1) * per, others)

    send_rows(0, x_send, x_in, *share(X_STEPS, 0))
    x_in[mine, :] = x_send[mine, :]

    gate_of[...] = jnp.sum(weighted, axis=1, keepdims=True)

    def gather_g(c, carry):
        at = pl.ds(pl.multiple_of(c * block, block), block)
        g_send[:, at] = (
            dot(place[...], out_grad[:, at], ((1,), (0,))) * gate_of[...]
        ).astype(BF16)
        return carry

    lax.fori_loop(0, width // block, gather_g, 0)
    g_in[mine, :] = g_send[mine, :]

    def gather_copy(way, k, ch):
        at = zone(dp - k if way == 0 else dp + k, ch, part_rows)
        remote(
            weights.at[at],
            weights.at[at],
            ag_s.at[way, k, ch],
            ag_r.at[way, k, ch],
            (right if way == 0 else left, me),
        )

    def gathered(way, k, ch):
        z = dp - k - 1 if way == 0 else dp + k + 1
        await_bytes(weights.at[zone(z, ch, part_rows)], ag_r.at[way, k, ch])

    arrived(0)
    for ch in range(CHUNKS):
        for way in (0, 1):
            gather_copy(way, 0, ch)

    for k in range(1, X_STEPS):
        send_rows(0, x_send, x_in, *share(X_STEPS, k))

    def gather_step(k, carry):
        for ch in range(CHUNKS):
            for way in (0, 1):
                gathered(way, k, ch)

                if on_far(way, ch):
                    gather_copy(way, k + 1, ch)
                else:

                    @pl.when(k + 1 < half - 1)
                    def _():
                        gather_copy(way, k + 1, ch)

        @pl.when(k < G_STEPS)
        def _():
            send_rows(1, g_send, g_in, *share(G_STEPS, k))

        return carry

    lax.fori_loop(0, half - 1, gather_step, 0)
    for k in range(half - 1, G_STEPS):
        send_rows(1, g_send, g_in, *share(G_STEPS, k))

    for load in loads:
        load.wait()
    moment_hop_one(1, moments_old.at[0])
    moment_hop_one(2, moments_old.at[1])

    weighted_t = weighted.T
    high = weighted_t.astype(BF16)
    high_t[...] = high
    low_t[...] = (weighted_t - high.astype(F32)).astype(BF16)
    place_t[...] = spread.T.astype(BF16)

    def hidden_sums(rows_here, base, zs, first):
        step = min(256, hid) if base == 0 else hid
        for c in range(base, 2 * hid if base == 0 else 3 * hid, step):
            total = None
            for z in zs:
                term = dot(
                    jnp.concatenate([rows_here[:, zone(i)] for i in z], axis=1),
                    jnp.concatenate([weights[zone(i), c : c + step] for i in z], axis=0),
                    ((1,), (0,)),
                )
                total = term if total is None else total + term
            gate_up[:, c : c + step] = total if first else gate_up[:, c : c + step] + total

    near = [dp + half + 1 + n for n in range(groups - 1)]
    near = [near[n : n + 2] for n in range(0, groups - 1, 2)]
    rows_arrived(0, x_in)
    hidden_sums(x_in, 0, near, True)
    rows_arrived(1, g_in)
    hidden_sums(g_in, 2 * hid, near, True)
    moment_hop_two(1, moments.at[0], 0)
    moment_hop_two(2, moments.at[1], 0)
    for ch in range(CHUNKS):
        gathered(0 if on_far(0, ch) else 1, half - 1, ch)
    hidden_sums(x_in, 0, [[dp + half]], False)

    height = min(64, slots)

    def each_part(body):
        def step(c, carry):
            body(pl.ds(pl.multiple_of(c * height, height), height))
            return carry

        lax.fori_loop(0, slots // height, step, 0)

    def forward(at):
        gate = gate_up[at, 0:hid]
        act[at, :] = (gate * jax.nn.sigmoid(gate) * gate_up[at, hid : 2 * hid]).astype(BF16)

    each_part(forward)

    def route_out(c, carry):
        at = pl.ds(pl.multiple_of(c * block, block), block)
        ro_send[:, at] = dot(act[...], weights[at, 2 * hid : 3 * hid], ((1,), (1,))).astype(BF16)
        return carry

    lax.fori_loop(0, width // block, route_out, 0)
    send_rows(2, ro_send, ro_in, 1, experts)
    ro_in[mine, :] = ro_send[mine, :]

    hidden_sums(g_in, 2 * hid, [[dp + half]], False)

    def backward(at):
        gate = gate_up[at, 0:hid]
        up = gate_up[at, hid : 2 * hid]
        grad = gate_up[at, 2 * hid : 3 * hid]
        sig = jax.nn.sigmoid(gate)
        pre[at, 0:hid] = (grad * up * sig * (1.0 + gate * (1.0 - sig))).astype(BF16)
        pre[at, hid : 2 * hid] = (grad * (gate * sig)).astype(BF16)

    each_part(backward)

    def partial(*zs):
        x_side = jnp.concatenate([x_in[:, zone(z)] for z in zs], axis=1)
        g_side = jnp.concatenate([g_in[:, zone(z)] for z in zs], axis=1)
        high = len(zs) * rows
        part[0:high, 0 : 2 * hid] = dot(x_side, pre[...], ((0,), (0,)))
        part[0:high, 2 * hid : 3 * hid] = dot(g_side, act[...], ((0,), (0,)))

    def sum_copy(way, k, ch):
        at = pl.ds(ch * part_rows, part_rows)
        remote(
            sum_send.at[way, k, at],
            sum_in.at[way, k, at],
            rs_s.at[way, k, ch],
            rs_r.at[way, k, ch],
            (right if way == 0 else left, me),
        )

    def sum_arrived(way, k, ch):
        at = pl.ds(ch * part_rows, part_rows)
        await_bytes(sum_in.at[way, k, at], rs_r.at[way, k, ch])

    partial(dp + half)
    for ch in range(CHUNKS):
        way = 0 if on_far(0, ch) else 1
        at = pl.ds(ch * part_rows, part_rows)
        sum_send[way, 0, at] = part[at, :].astype(BF16)
        sum_copy(way, 0, ch)

    def sum_step(k, carry):
        partial(dp + half - k, dp - half + k)

        for ch in range(CHUNKS):
            at = pl.ds(ch * part_rows, part_rows)
            for way in (0, 1):
                own = pl.ds(way * rows + ch * part_rows, part_rows)

                def add():
                    sum_arrived(way, k - 1, ch)
                    sum_send[way, k, at] = (
                        part[own, :] + sum_in[way, k - 1, at].astype(F32)
                    ).astype(BF16)

                if on_far(way, ch):
                    add()
                else:
                    pl.when(k > 1)(add)

                    @pl.when(k == 1)
                    def _():
                        sum_send[way, k, at] = part[own, :].astype(BF16)

                sum_copy(way, k, ch)
        return carry

    def give_dx():
        def dx_out(c, carry):
            at = pl.ds(pl.multiple_of(c * block, block), block)
            dx_send[:, at] = dot(pre[...], weights[at, 0 : 2 * hid], ((1,), (1,))).astype(BF16)
            return carry

        lax.fori_loop(0, width // block, dx_out, 0)
        send_rows(3, dx_send, dx_in, 1, experts)
        dx_in[mine, :] = dx_send[mine, :]

    lax.fori_loop(1, 2, sum_step, 0)
    give_dx()
    lax.fori_loop(2, half, sum_step, 0)
    partial(dp)

    rows_arrived(2, ro_in)

    def combine(c, total):
        at = pl.ds(pl.multiple_of(c * block, block), block)
        rows_here = ro_in[:, at]
        moe_out[:, at] = (
            dot(high_t[...], rows_here, ((1,), (0,))) + dot(low_t[...], rows_here, ((1,), (0,)))
        ).astype(BF16)
        return total + dot(rows_here, out_grad[:, at], ((1,), (1,)))

    products = lax.fori_loop(0, width // block, combine, jnp.zeros((slots, tok), F32))
    for r in range(3):
        gate_grads[r : r + 1, :] = jnp.sum(
            jnp.where(slot_row == target[r], products, 0.0), axis=0, keepdims=True
        )
    moment_arrived(1)
    moment_arrived(2)
    w_moved[...] = weights[zone(dp), :]
    m_moved[...] = moments[0]
    v_moved[...] = moments[1]
    for ch in range(CHUNKS):
        at = pl.ds(ch * part_rows, part_rows)
        for way in (0, 1):
            sum_arrived(way, half - 1, ch)
        grad_sum[at, :] = (
            part[at, :]
            + sum_in[0, half - 1, at].astype(F32)
            + sum_in[1, half - 1, at].astype(F32)
        )

    rows_arrived(3, dx_in)

    def combine_dx(c, carry):
        at = pl.ds(pl.multiple_of(c * block, block), block)
        tokens_grad[:, at] = dot(place_t[...], dx_in[:, at], ((1,), (0,))).astype(BF16)
        return carry

    lax.fori_loop(0, width // block, combine_dx, 0)

    for n, ref in enumerate((x_send, g_send, ro_send, dx_send)):
        await_bytes(ref.at[pl.ds(0, others * SLOT)], a2a_s.at[n])
    hops_sent(0)
    for a in (1, 2):
        moment_hops_sent(a)
    for ch in range(CHUNKS):
        at = pl.ds(ch * part_rows, part_rows)
        for way in (0, 1):

            def left_here(k, carry):
                await_bytes(sum_send.at[way, k, at], ag_s.at[way, k, ch])
                await_bytes(sum_send.at[way, k + 1, at], rs_s.at[way, k + 1, ch])
                return carry

            lax.fori_loop(0, half - 1, left_here, 0)
        way = 0 if on_far(0, ch) else 1
        await_bytes(sum_send.at[way, half - 1, at], ag_s.at[way, half - 1, ch])
        await_bytes(sum_send.at[way, 0, at], rs_s.at[way, 0, ch])


def shards(
    grid,
    tokens,
    route_gates,
    expert_ids,
    owner_now,
    owner_next,
    out_grad,
    expert_weights,
    first_moment,
    second_moment,
):
    groups, experts = lax.axis_size("dp"), lax.axis_size("expert")
    tok, width = tokens.shape
    _, rows, cols = expert_weights.shape
    hid = cols // 3
    slots = experts * SLOT
    half = groups // 2
    matches = owner_next[None, :] == jnp.arange(experts, dtype=jnp.int32)[:, None]
    source = jnp.sum(jnp.where(matches, owner_now[None, :], 0), axis=1)
    vmem = pl.BlockSpec(memory_space=pltpu.VMEM)
    dma = pltpu.SemaphoreType.DMA
    state = jax.ShapeDtypeStruct((rows, cols), BF16)
    result = pl.pallas_call(
        functools.partial(kernel, (groups, experts, *grid)),
        out_shape=(
            jax.ShapeDtypeStruct((tok, width), BF16),
            jax.ShapeDtypeStruct((tok, width), BF16),
            jax.ShapeDtypeStruct(route_gates.shape[::-1], F32),
            jax.ShapeDtypeStruct((rows, cols), F32),
            state,
            state,
            state,
        ),
        in_specs=[pl.BlockSpec(memory_space=pltpu.SMEM)]
        + [vmem] * 6
        + [pl.BlockSpec(memory_space=pl.ANY)] * 2,
        out_specs=(vmem,) * 7,
        scratch_shapes=[
            pltpu.VMEM((slots, width), BF16),
            pltpu.VMEM((slots, width), BF16),
            pltpu.VMEM((slots, width), BF16),
            pltpu.VMEM((slots, width), BF16),
            pltpu.VMEM((width, cols), BF16),
            pltpu.VMEM((slots, cols), F32),
            pltpu.VMEM((slots, hid), BF16),
            pltpu.VMEM((slots, 2 * hid), BF16),
            pltpu.VMEM((slots, width), BF16),
            pltpu.VMEM((slots, width), BF16),
            pltpu.VMEM((slots, width), BF16),
            pltpu.VMEM((slots, width), BF16),
            pltpu.VMEM((2, half, rows, cols), BF16),
            pltpu.VMEM((2, half, rows, cols), BF16),
            pltpu.VMEM((2 * rows, cols), F32),
            pltpu.VMEM((slots, tok), BF16),
            pltpu.VMEM((tok, slots), BF16),
            pltpu.VMEM((tok, slots), BF16),
            pltpu.VMEM((tok, slots), BF16),
            pltpu.VMEM((slots, 1), F32),
            pltpu.VMEM((experts, SLOT, WIDE), BF16),
            pltpu.VMEM((experts, SLOT, NARROW), BF16),
            pltpu.VMEM((experts, SLOT, WIDE), BF16),
            pltpu.VMEM((experts, SLOT, NARROW), BF16),
            *[pltpu.VMEM((experts, SLOT, cols), BF16)] * 4,
            pltpu.VMEM((2, rows, cols), BF16),
            pltpu.VMEM((2, rows, cols), BF16),
            dma((2,)),
            dma((4,)),
            dma((4,)),
            dma((3, 2)),
            dma((3, 2)),
            dma((3, 2)),
            dma((3, 2)),
            dma((2, half, CHUNKS)),
            dma((2, half, CHUNKS)),
            dma((2, half, CHUNKS)),
            dma((2, half, CHUNKS)),
        ],
        compiler_params=pltpu.CompilerParams(
            collective_id=0, has_side_effects=True, vmem_limit_bytes=60 * 2**20
        ),
        name="moe_step",
    )(
        source,
        tokens,
        route_gates.T,
        expert_ids.T,
        owner_next[None, :],
        out_grad,
        expert_weights[0],
        first_moment[0],
        second_moment[0],
    )
    moe_out, tokens_grad, gate_grads, grad, w_old, m_old, v_old = result
    first = beta_one * m_old.astype(F32) + (1.0 - beta_one) * grad
    second = beta_two * v_old.astype(F32) + (1.0 - beta_two) * grad * grad
    w_new = w_old.astype(F32) - learn_rate * first / (jnp.sqrt(second) + adam_eps)
    return (
        moe_out,
        tokens_grad,
        gate_grads.T,
        w_new.astype(BF16)[None],
        first.astype(BF16)[None],
        second.astype(BF16)[None],
    )


def solution(mesh):
    pairs = mesh.shape["expert"] // 2
    ys = 1
    while ys * ys * 4 <= pairs:
        ys *= 2
    by_token = P(("dp", "expert"), None)
    by_state = P("expert", "dp", None)
    return jax.shard_map(
        functools.partial(shards, (pairs // ys, ys)),
        mesh=mesh,
        in_specs=(by_token,) * 3 + (P(), P()) + (by_token,) + (by_state,) * 3,
        out_specs=(by_token,) * 3 + (by_state,) * 3,
        check_vma=False,
    )
```
